512 devices in a mesh: src: 4 (over x), gx: 8 (over y_lo, core), gy: 16 (over z, y_hi).
Axes of the slice: x: 4, y: 8 (y_hi: 2, y_lo: 4; y = y_hi * 4 + y_lo), z: 8, core: 2. Of those that a mesh axis runs over, the one named last changes fastest.
Arguments:
- cam_send: bfloat16 [32, 16, 32, 2, 16, 256], P(('src', 'gx'), 'gy'), may hold values from -6 to 6
- lidar_bev: bfloat16 [4, 128, 1024, 256], P('src', 'gx', 'gy'), may hold values from -6 to 6
- tile_active: int32 [4, 32, 256], P('src', 'gx', 'gy'), may hold values 0 or 1
- tile_source: int32 [4, 32, 256], P('src', 'gx', 'gy'), may hold values from 0 to 63, as said below
- conv_weight: bfloat16 [3, 3, 256, 256], replicated, may hold values from -0.125 to 0.125
- head_up: bfloat16 [256, 512], replicated, may hold values from -0.375 to 0.375
- head_out: bfloat16 [512, 128], replicated, may hold values from -0.25 to 0.25
- cotangent: bfloat16 [4, 128, 1024, 128], P('src', 'gx', 'gy'), may hold values from -6 to 6
Outputs:
- head_maps: bfloat16 [4, 128, 1024, 128], P('src', 'gx', 'gy')
- grad_lidar: bfloat16 [4, 128, 1024, 256], P('src', 'gx', 'gy')
- grad_cam: bfloat16 [32, 16, 32, 2, 16, 256], P(('src', 'gx'), 'gy')
- grad_conv: float32 [589824], P(('src', 'gx', 'gy'))
- grad_up: float32 [256, 512], replicated
- grad_out: float32 [512, 128], replicated
The draws below stay inside these ranges and needn't reach their ends.
Inputs may be any that keep to these rules, and one draw needn't show every extreme that they name: `tile_source`: within the 4 x 16 tiles of one sample that fall on one grid device, the values are distinct and take every value of the range; value // 2 is the camera section (index of src+gx) holding the tile, value % 2 its slot.
All inputs are finite; a program needn't handle non-finite values. No bound on the sum of `tile_active` on one device may be relied on, other than what follows from the above.
Results may differ from the reference program's by a relative error of at most 0.007.
Values may be sent and summed in bfloat16 or wider, within the bound.
A program may use at most 64 MiB of HBM per device.

```python
import math
import jax
import jax.numpy as jnp
from jax import lax

C = 256
HEAD = 512
OUTC = 128
TS = 4
TX = 4
TY = 16
CAP = 2
NTX = 32
NTY = 256
NX = 128
NY = 1024
N_SRC = 4
N_GX = 8
N_GY = 16


def draw_tile_source(key, part):
    key = jax.random.fold_in(key, 11)
    sources = N_SRC * N_GX
    slots_all = sources * CAP
    per_device = TX * TY
    blocks = N_SRC * N_GX * N_GY
    block_keys = jax.random.split(key, blocks)

    def one_block(block_key):
        key_slots, key_tiles = jax.random.split(block_key)
        shuffled = jax.random.permutation(key_slots, slots_all).astype(jnp.int32)
        busiest = shuffled[0] // CAP
        position = jnp.arange(slots_all, dtype=jnp.int32)
        score = jnp.where(shuffled // CAP == busiest, shuffled % CAP - CAP, position)
        ranked = shuffled[jnp.argsort(score)]
        chosen = ranked[:per_device]
        return chosen[jax.random.permutation(key_tiles, per_device)]
    assigned = jax.vmap(one_block)(block_keys)
    assigned = assigned.reshape(N_SRC, N_GX, N_GY, TX, TY).transpose(0, 1, 3, 2, 4)
    return assigned.reshape(N_SRC, N_GX * TX, N_GY * TY).astype(jnp.int32)


def place_ends(array, stream_key, least, largest):
    longest = array.shape.index(max(array.shape))
    spots = []
    for shift in (0, 1):
        where = [jax.random.randint(jax.random.fold_in(stream_key, axis), (), 0, length) for axis, length in enumerate(array.shape)]
        where[longest] = (where[longest] + shift) % array.shape[longest]
        spots.append(tuple(where))
    return array.at[spots[0]].set(least).at[spots[1]].set(largest)


def shard_levels(stream_key, dims, shards, least, largest):
    def one(dim, blocks):
        steps = jax.random.uniform(jax.random.fold_in(jax.random.fold_in(stream_key, 6), dim), (blocks,), jnp.float32, least / len(shards), largest / len(shards))
        return jnp.repeat(jnp.exp(steps), dims[dim] // blocks).reshape((-1,) + (1,) * (len(dims) - dim - 1))

    level = one(*shards[0])
    for cut in shards[1:]:
        level = level * one(*cut)
    return level


def scatter_about(rng, dims, scale, limit, cuts=(), kind=jnp.bfloat16):
    entries = scale * jax.random.normal(rng, dims, jnp.float32)
    if cuts:
        entries = entries * shard_levels(rng, dims, cuts, -0.22, 0.18)
    return jnp.clip(entries, -limit, limit).astype(kind)


def setup_inputs(seed: int = 0) -> dict:
    key_list = jax.random.split(jax.random.key(seed), 9)
    cam_send = scatter_about(key_list[0], (N_SRC * N_GX, N_GY, N_SRC * N_GX, CAP, TS * TS, C), 1.0, 6.0, ((0, 32), (1, 16)))
    lidar_bev = scatter_about(key_list[1], (N_SRC, NX, NY, C), 1.0, 6.0, ((0, 4), (1, 8), (2, 16)))
    tile_active = place_ends((jax.random.randint(key_list[2], (N_SRC, NTX, NTY), 0, 4) < 3).astype(jnp.int32), jax.random.fold_in(key_list[2], 1), 0, 1)
    tile_source = draw_tile_source(jax.random.fold_in(key_list[8], 71), 0)
    conv_weight = scatter_about(key_list[4], (3, 3, C, C), (9 * C) ** -0.5, 0.125)
    head_up = scatter_about(key_list[5], (C, HEAD), C ** -0.5, 0.375)
    head_out = scatter_about(key_list[6], (HEAD, OUTC), HEAD ** -0.5, 0.25)
    cotangent = scatter_about(key_list[7], (N_SRC, NX, NY, OUTC), 1.0, 6.0, ((0, 4), (1, 8), (2, 16)))
    return dict(cam_send=cam_send, lidar_bev=lidar_bev, tile_active=tile_active, tile_source=tile_source, conv_weight=conv_weight, head_up=head_up, head_out=head_out, cotangent=cotangent)


def silu_slope(value):
    sigmoid_value = jax.nn.sigmoid(value)
    return sigmoid_value * (1.0 + value * (1.0 - sigmoid_value))

def conv_taps(padded, weight, cells_x, cells_y):
    channels = weight.shape[2]
    summed = jnp.zeros((cells_x * cells_y, weight.shape[3]), jnp.float32)
    for row_tap in range(3):
        for col_tap in range(3):
            window = padded[row_tap:row_tap + cells_x, col_tap:col_tap + cells_y].reshape(cells_x * cells_y, channels)
            summed = summed + jnp.dot(window, weight[row_tap, col_tap], preferred_element_type=jnp.float32)
    return summed

def conv_back(padded, weight, cells_x, cells_y):
    channels = weight.shape[3]
    summed = jnp.zeros((cells_x * cells_y, weight.shape[2]), jnp.float32)
    for row_tap in range(3):
        for col_tap in range(3):
            window = padded[2 - row_tap:2 - row_tap + cells_x, 2 - col_tap:2 - col_tap + cells_y].reshape(cells_x * cells_y, channels)
            summed = summed + jnp.dot(window, weight[row_tap, col_tap].T, preferred_element_type=jnp.float32)
    return summed

def tap_grads(padded, grad_pre, cells_x, cells_y):
    channels = padded.shape[-1]
    rows_list = []
    for row_tap in range(3):
        row_items = []
        for col_tap in range(3):
            window = padded[row_tap:row_tap + cells_x, col_tap:col_tap + cells_y].reshape(cells_x * cells_y, channels)
            row_items.append(jnp.dot(window.T, grad_pre, preferred_element_type=jnp.float32))
        rows_list.append(jnp.stack(row_items))
    return jnp.stack(rows_list)

def reference(cam_send, lidar_bev, tile_active, tile_source, conv_weight, head_up, head_out, cotangent):
    tiles_x = TX * N_GX
    tiles_y = TY * N_GY
    scale = 1.0 / math.sqrt(N_SRC * NX * NY)
    sender = tile_source // CAP
    slot_index = tile_source % CAP
    batch_index = jnp.arange(N_SRC, dtype=jnp.int32)[:, None, None]
    tile_xs = jnp.arange(tiles_x, dtype=jnp.int32)[None, :, None]
    tile_ys = jnp.arange(tiles_y, dtype=jnp.int32)[None, None, :]
    dest = jnp.broadcast_to(batch_index * N_GX + tile_xs // TX, tile_source.shape)
    row_dev = jnp.broadcast_to(tile_ys // TY, tile_source.shape)
    cam_tiles = cam_send[sender, row_dev, dest, slot_index]
    camera = cam_tiles.reshape(N_SRC, tiles_x, tiles_y, TS, TS, C).transpose(0, 1, 3, 2, 4, 5).reshape(N_SRC, NX, NY, C)
    occupied = jnp.broadcast_to(tile_active.astype(jnp.float32)[:, :, None, :, None], (N_SRC, tiles_x, TS, tiles_y, TS)).reshape(N_SRC, NX, NY)

    def sample(items):
        cam_one, lidar_one, mask_one, upstream = items
        mask_flat = mask_one.reshape(NX * NY, 1)
        merged = (mask_one[:, :, None] * (cam_one.astype(jnp.float32) + lidar_one.astype(jnp.float32))).astype(jnp.bfloat16)
        padded = jnp.pad(merged, ((1, 1), (1, 1), (0, 0)))
        pre_act = conv_taps(padded, conv_weight, NX, NY)
        feature = (mask_flat * jax.nn.silu(pre_act)).astype(jnp.bfloat16)
        up_act = jnp.dot(feature, head_up, preferred_element_type=jnp.float32)
        hidden = jax.nn.silu(up_act).astype(jnp.bfloat16)
        head_one = jnp.dot(hidden, head_out, preferred_element_type=jnp.float32).astype(jnp.bfloat16)
        upstream_flat = upstream.reshape(NX * NY, OUTC)
        out_term = jnp.dot(hidden.T, upstream_flat, preferred_element_type=jnp.float32)
        grad_hidden = (jnp.dot(upstream_flat, head_out.T, preferred_element_type=jnp.float32) * silu_slope(up_act)).astype(jnp.bfloat16)
        up_term = jnp.dot(feature.T, grad_hidden, preferred_element_type=jnp.float32)
        grad_feat = jnp.dot(grad_hidden, head_up.T, preferred_element_type=jnp.float32)
        grad_pre = (mask_flat * grad_feat * silu_slope(pre_act)).astype(jnp.bfloat16)
        conv_term = tap_grads(padded, grad_pre, NX, NY)
        grad_padded = jnp.pad(grad_pre.reshape(NX, NY, C), ((1, 1), (1, 1), (0, 0)))
        grad_merged = conv_back(grad_padded, conv_weight, NX, NY)
        grad_in = (mask_flat * grad_merged).astype(jnp.bfloat16).reshape(NX, NY, C)
        return (head_one.reshape(NX, NY, OUTC), grad_in, conv_term, up_term, out_term)
    head_maps, grad_lidar, conv_terms, up_terms, out_terms = lax.map(sample, (camera, lidar_bev, occupied, cotangent))
    grad_tiles = grad_lidar.reshape(N_SRC, tiles_x, TS, tiles_y, TS, C).transpose(0, 1, 3, 2, 4, 5).reshape(N_SRC, tiles_x, tiles_y, TS * TS, C)
    grad_cam = jnp.zeros_like(cam_send).at[sender, row_dev, dest, slot_index].set(grad_tiles)
    grad_conv = (lax.optimization_barrier(jnp.sum(conv_terms, axis=0)) * scale).reshape(9 * C * C)
    grad_up = lax.optimization_barrier(jnp.sum(up_terms, axis=0)) * scale
    grad_out = lax.optimization_barrier(jnp.sum(out_terms, axis=0)) * scale
    return (head_maps, grad_lidar, grad_cam, grad_conv, grad_up, grad_out)
```

```python
import functools
import math

import jax
import jax.numpy as jnp
from jax import lax
from jax.experimental import pallas as pl
from jax.experimental.pallas import tpu as pltpu
from jax.sharding import PartitionSpec as P

MESH = pl.DeviceIdType.MESH
F32 = jnp.float32
BF16 = jnp.bfloat16


def pad16(rows):
    return (rows + 15) // 16 * 16


def sigmoid(value):
    return 0.5 * jnp.tanh(0.5 * value) + 0.5


def dot(lhs, rhs):
    return jnp.dot(lhs, rhs, preferred_element_type=F32)


def dot_tn(lhs, rhs):
    return lax.dot_general(lhs, rhs, (((0,), (0,)), ((), ())), preferred_element_type=F32)


def rcopy(src, dst, send_sem, recv_sem, device):
    return pltpu.make_async_remote_copy(
        src_ref=src,
        dst_ref=dst,
        send_sem=send_sem,
        recv_sem=recv_sem,
        device_id=device,
        device_id_type=MESH,
    )


class Dims:
    def __init__(self, n_src, n_gx, n_gy, cells_x, cells_y, channels, head, outc):
        self.X, self.GX, self.GY = n_src, n_gx, n_gy
        self.YL, self.Z, self.Y = n_gx // 2, n_gy // 2, n_gx
        self.N = n_src * n_gx
        self.cx, self.cy, self.c = cells_x, cells_y, channels
        self.cells = cells_x * cells_y
        self.tx, self.ty = cells_x // 4, cells_y // 4
        self.tiles = self.tx * self.ty
        self.head, self.outc = head, outc
        self.colp = pad16(cells_x)
        self.rows = 9 * channels
        self.rc = self.rows // 2
        self.rz = self.rc // self.Z
        self.rx = self.rz // self.X
        self.rxp = pad16(self.rx)
        self.hb = 2 * self.rx // self.Y
        self.hbp = pad16(self.hb)
        self.hrows = (channels * head + head * outc) // channels
        self.hc = self.hrows // 2
        self.hx = self.hc // self.X
        self.hz = self.hx // self.Z
        self.hzp = pad16(self.hz)
        self.scale = 1.0 / math.sqrt(n_src * n_gx * n_gy * cells_x * cells_y)


def kernel(
    d,
    cam, lidar_h, act, tsrc, inv, wconv_h, hup_h, hout_h, cot_h,
    maps_o, gin_o, gcam_o, gconv_o, gup_o, gout_o,
    arrived, lidar, wconv, hup, hout, cot,
    wt, hup_t, hout_t, mask,
    m32, m3, g3, rows_s, rows_r, cols_s, cols_r,
    feat, hid, gh, maps, gp, gi, tiles, ret,
    dw32, dwb, core_r, cs32, zs, z_r, zsum, xs32, xsb, x_r, hrow, ls, l_r,
    h32, hb, hcore_r, hs32, hxs, hx_r, hxsum, hzs32, hzs, hz_r, hy, hy_r, hall,
    in_sem, out_sem,
    a_send, a_recv, b_send, b_recv,
    halo_send, halo_recv, core_send, core_recv,
    z_send, z_recv, x_send, x_recv, l_send, l_recv,
    hx_send, hx_recv, hz_send, hz_recv, hy_send, hy_recv,
    gz_send, gz_recv, gx_send, gx_recv,
):
    s = lax.axis_index("src")
    g = lax.axis_index("gx")
    r = lax.axis_index("gy")
    core, yl = g % 2, g // 2
    z, yh = r // 2, r % 2
    me = s * d.GX + g
    X, Y, Z, N, C, CY = d.X, d.Y, d.Z, d.N, d.c, d.cy

    loads = [
        pltpu.make_async_copy(src, dst, in_sem.at[k])
        for k, (src, dst) in enumerate(
            [(lidar_h, lidar), (wconv_h, wconv), (hup_h, hup), (hout_h, hout), (cot_h, cot),
             (cam.at[me], arrived.at[me])]
        )
    ]
    for load in loads:
        load.start()

    def a_peer(step):
        other = (me + step) % N
        return (other // d.GX, other % d.GX, r)

    def z_peer(step):
        return (s, g, ((z + step) % Z) * 2 + yh)

    def x_peer(step):
        return ((s + step) % X, g, r)

    def y_peer(step):
        at = (yl * 2 + yh + step) % Y
        return (s, (at // 2) * 2 + core, z * 2 + at % 2)

    other_core = (s, yl * 2 + 1 - core, r)

    block0 = ((core * Z + z) * X + s) * Y
    my_block = (s * d.GX + g) * d.GY + r
    group = my_block // Y
    from_core, from_z, from_x = group // (Z * X), (group // X) % Z, group % X

    def owner(block):
        at = block0 + block
        return (at // (d.GX * d.GY), (at // d.GY) % d.GX, at % d.GY)

    def last_sender(at):
        return (from_x, (at // 2) * 2 + from_core, from_z * 2 + at % 2)

    self_group = jnp.logical_and(
        jnp.logical_and(from_core == core, from_z == z), from_x == s
    )
    my_y = yl * 2 + yh

    barrier = pltpu.get_barrier_semaphore()

    def greet(device):
        pl.semaphore_signal(barrier, inc=1, device_id=device, device_id_type=MESH)

    def greet_a(step, _):
        greet(a_peer(step))
        return 0

    lax.fori_loop(1, N, greet_a, 0)
    count = N - 1
    for step in range(1, Z):
        greet(z_peer(step))
        count += 1
    for at in range(d.YL):
        greet((s, at * 2 + core, z * 2 + 1 - yh))
        count += 1
    for side in (-1, 1):
        for near in (-1, 0, 1):
            greet((s, (g + near + d.GX) % d.GX, (r + side + d.GY) % d.GY))
            count += 1
    for at in range(Y):
        is_self = jnp.logical_and(self_group, my_y == at)

        @pl.when(jnp.logical_not(is_self))
        def _():
            greet(last_sender(at))

    count = count + Y - jnp.where(self_group, 1, 0)
    pl.semaphore_wait(barrier, count)

    def a_copy(step):
        return rcopy(
            cam.at[(me + step) % N], arrived.at[me], a_send.at[step], a_recv.at[step], a_peer(step)
        )

    def a_start(step, _):
        a_copy(step).start()
        return 0

    lax.fori_loop(1, N, a_start, 0)

    for load in loads[:5]:
        load.wait()
    at_y = lax.broadcasted_iota(jnp.int32, (CY, d.ty), 0) // 4
    at_q = lax.broadcasted_iota(jnp.int32, (CY, d.ty), 1)
    for p in range(d.tx):
        row = act[p : p + 1, :].astype(F32)
        column = jnp.sum(jnp.where(at_y == at_q, row, 0.0), axis=1, keepdims=True)
        mask[p] = jnp.broadcast_to(column, (CY, C))
    for i in range(3):
        for j in range(3):
            tap = wconv[2 - i, (2 - j) * C : (3 - j) * C, :].astype(F32)
            wt[i, j * C : (j + 1) * C, :] = tap.T.astype(BF16)
    hup_t[...] = hup[...].astype(F32).T.astype(BF16)
    hout_t[...] = hout[...].astype(F32).T.astype(BF16)

    def a_wait(step, _):
        sender = (me - step + N) % N
        rcopy(
            cam.at[sender], arrived.at[sender], a_send.at[step], a_recv.at[step], a_peer(step)
        ).wait_recv()
        return 0

    lax.fori_loop(1, N, a_wait, 0)
    loads[5].wait()

    span = 4 * CY

    def merge(p, _):
        for q in range(d.ty):
            at = tsrc[p, q]
            tile = arrived[at // 2, at % 2].astype(F32)
            for dx in range(4):
                m32[4 * p + dx, 4 * q : 4 * q + 4, :] = tile[4 * dx : 4 * dx + 4]
        for dx in range(4):
            x = 4 * p + dx
            line = pl.ds(pl.multiple_of(x * CY, CY), CY)
            m32[x] = mask[p] * (m32[x] + lidar[line, :].astype(F32))
        return 0

    lax.fori_loop(0, d.tx, merge, 0)

    def halo_copies(k):
        copies = []
        for side, step in ((0, -1), (1, 1)):
            copies.append(
                (rows_s.at[k, side], rows_r.at[k, 1 - side], (s, (g + step + d.GX) % d.GX, r))
            )
            for near in (-1, 0, 1):
                device = (s, (g + near + d.GX) % d.GX, (r + step + d.GY) % d.GY)
                copies.append((cols_s.at[k, side], cols_r.at[k, 1 - side, 1 - near], device))
        return [
            rcopy(src, dst, halo_send.at[k, n], halo_recv.at[k, n], device)
            for n, (src, dst, device) in enumerate(copies)
        ]

    def halo_start(k):
        rows_s[k, 0] = m32[0].astype(BF16)
        rows_s[k, 1] = m32[d.cx - 1].astype(BF16)
        cols_s[k, 0, 0 : d.cx, :] = m32[:, 0, :].astype(BF16)
        cols_s[k, 1, 0 : d.cx, :] = m32[:, CY - 1, :].astype(BF16)
        copies = halo_copies(k)
        for copy in copies:
            copy.start()
        return copies

    def halo_finish(k, copies, out3):
        for copy in copies:
            copy.wait_recv()
        at = lax.broadcasted_iota(jnp.int32, (CY, C), 0)
        ok_g = (g > 0, g < d.GX - 1)
        ok_r = (r > 0, r < d.GY - 1)

        def put(x, line, left, right):
            down = jnp.where(at == 0, left, pltpu.roll(line, 1, 0))
            up = jnp.where(at == CY - 1, right, pltpu.roll(line, CY - 1, 0))
            out3[x * CY : (x + 1) * CY, 0:C] = down.astype(BF16)
            out3[x * CY : (x + 1) * CY, C : 2 * C] = line.astype(BF16)
            out3[x * CY : (x + 1) * CY, 2 * C : 3 * C] = up.astype(BF16)

        def column(side, near, x, ok):
            value = cols_r[k, side, near].astype(F32)[x : x + 1]
            return jnp.where(ok, value, 0.0)

        for x in range(d.cx):
            left = column(0, 1, x, ok_r[0])
            right = column(1, 1, x, ok_r[1])
            put(x + 1, m32[x], left, right)
        for side, x, row in ((0, 0, d.cx - 1), (1, d.cx + 1, 0)):
            line = jnp.where(ok_g[side], rows_r[k, side].astype(F32), 0.0)
            near = 0 if side == 0 else 2
            left = column(0, near, row, jnp.logical_and(ok_g[side], ok_r[0]))
            right = column(1, near, row, jnp.logical_and(ok_g[side], ok_r[1]))
            put(x, line, left, right)

    halo0 = halo_start(0)
    halo_finish(0, halo0, m3)

    def forward(p, _):
        here = pl.ds(pl.multiple_of(p * span, span), span)
        pre = jnp.zeros((span, C), F32)
        for i in range(3):
            pre = pre + dot(
                m3[pl.ds(pl.multiple_of(p * span + i * CY, CY), span), :], wconv[i]
            )
        occupied = jnp.concatenate([mask[p]] * 4, axis=0)
        sig = sigmoid(pre)
        feature = (occupied * (pre * sig)).astype(BF16)
        slope = occupied * (sig * (1.0 + pre * (1.0 - sig)))
        feat[here, :] = feature
        lines = pl.ds(4 * p, 4)
        m32[lines] = slope.reshape(4, CY, C)
        up = dot(feature, hup[...])
        sig = sigmoid(up)
        hidden = (up * sig).astype(BF16)
        hid[here, :] = hidden
        maps[here, :] = dot(hidden, hout[...]).astype(BF16)
        grad = (dot(cot[here, :], hout_t[...]) * (sig * (1.0 + up * (1.0 - sig)))).astype(BF16)
        gh[here, :] = grad
        value = dot(grad, hup_t[...]) * m32[lines].reshape(span, C)
        m32[lines] = value.reshape(4, CY, C)
        gp[here, :] = value.astype(BF16)
        return 0

    lax.fori_loop(0, d.tx, forward, 0)
    halo1 = halo_start(1)
    maps_out = pltpu.make_async_copy(maps, maps_o, out_sem.at[0])
    maps_out.start()

    def tap_grads(i, _):
        for j in range(3):
            term = dot_tn(
                m3[pl.ds(pl.multiple_of(i * CY, CY), d.cells), j * C : (j + 1) * C], gp[...]
            )
            at = pl.ds(pl.multiple_of(i * (3 * C) + j * C, C), C)
            dw32[at, :] = term
            dwb[at, :] = term.astype(BF16)
        return 0

    lax.fori_loop(0, 3, tap_grads, 0)
    mine = pl.ds(pl.multiple_of(core * d.rc, d.rc), d.rc)
    theirs = pl.ds(pl.multiple_of((1 - core) * d.rc, d.rc), d.rc)
    core_copy = rcopy(dwb.at[theirs], core_r, core_send.at[0], core_recv.at[0], other_core)
    core_copy.start()

    term = dot_tn(feat[...], gh[...])
    for half in range(d.head // C):
        h32[half * C : (half + 1) * C, :] = term[:, half * C : (half + 1) * C]
    base = d.head
    term = dot_tn(hid[...], cot[...])
    depth = d.head // 2
    for half in range(2):
        h32[base : base + depth, half * d.outc : (half + 1) * d.outc] = term[
            half * depth : (half + 1) * depth, :
        ]
    hb[...] = h32[...].astype(BF16)
    hmine = pl.ds(pl.multiple_of(core * d.hc, d.hc), d.hc)
    htheirs = pl.ds(pl.multiple_of((1 - core) * d.hc, d.hc), d.hc)
    hcore_copy = rcopy(hb.at[htheirs], hcore_r, core_send.at[1], core_recv.at[1], other_core)
    hcore_copy.start()

    core_copy.wait_recv()
    cs32[...] = dw32[mine, :] + core_r[...].astype(F32)
    for k in range(Z):
        zs[k] = cs32[k * d.rz : (k + 1) * d.rz, :].astype(BF16)
    z_copies = [
        rcopy(zs.at[(z + k) % Z], z_r.at[k - 1], z_send.at[k], z_recv.at[k], z_peer(k))
        for k in range(1, Z)
    ]
    for copy in z_copies:
        copy.start()

    hcore_copy.wait_recv()
    hs32[...] = h32[hmine, :] + hcore_r[...].astype(F32)
    for k in range(X):
        hxs[k] = hs32[k * d.hx : (k + 1) * d.hx, :].astype(BF16)
    hx_copies = [
        rcopy(hxs.at[(s + k) % X], hx_r.at[k - 1], hx_send.at[k], hx_recv.at[k], x_peer(k))
        for k in range(1, X)
    ]
    for copy in hx_copies:
        copy.start()

    halo_finish(1, halo1, g3)

    def backward(p, _):
        here = pl.ds(pl.multiple_of(p * span, span), span)
        acc = jnp.zeros((span, C), F32)
        for i in range(3):
            acc = acc + dot(g3[pl.ds(pl.multiple_of(p * span + i * CY, CY), span), :], wt[i])
        acc = acc * jnp.concatenate([mask[p]] * 4, axis=0)
        gi[here, :] = acc.astype(BF16)
        m32[pl.ds(4 * p, 4)] = acc.reshape(4, CY, C)
        for q in range(d.ty):
            parts = [m32[4 * p + dx, 4 * q : 4 * q + 4, :] for dx in range(4)]
            tiles[p * d.ty + q] = jnp.concatenate(parts, axis=0).astype(BF16)
        return 0

    lax.fori_loop(0, d.tx, backward, 0)
    gin_out = pltpu.make_async_copy(gi, gin_o, out_sem.at[1])
    gin_out.start()

    def b_copy(step):
        other = (me + step) % N
        return rcopy(
            ret.at[other], gcam_o.at[me], b_send.at[step], b_recv.at[step], a_peer(step)
        )

    def fill(other, _):
        for slot in range(2):
            ret[other, slot] = tiles[inv[other * 2 + slot]]
        return 0

    lax.fori_loop(0, N, fill, 0)

    def b_start(step, _):
        b_copy(step).start()
        return 0

    lax.fori_loop(1, N, b_start, 0)
    own_out = pltpu.make_async_copy(ret.at[me], gcam_o.at[me], out_sem.at[2])
    own_out.start()

    for copy in hx_copies:
        copy.wait_recv()
    total = hs32[pl.ds(pl.multiple_of(s * d.hx, d.hx), d.hx), :]
    for k in range(X - 1):
        total = total + hx_r[k].astype(F32)
    hxsum[0 : d.hx, :] = total
    for k in range(Z):
        part = hxsum[k * d.hz : k * d.hz + d.hzp, :]
        hzs32[k] = part
        hzs[k] = part.astype(BF16)
    hz_copies = [
        rcopy(hzs.at[(z + k) % Z], hz_r.at[k - 1], hz_send.at[k], hz_recv.at[k], z_peer(k))
        for k in range(1, Z)
    ]
    for copy in hz_copies:
        copy.start()
    for copy in hz_copies:
        copy.wait_recv()
    total = hzs32[z]
    for k in range(Z - 1):
        total = total + hz_r[k].astype(F32)
    hy[...] = total.astype(BF16)
    hy_copies = [
        rcopy(hy, hy_r.at[k - 1], hy_send.at[k], hy_recv.at[k], y_peer(k)) for k in range(1, Y)
    ]
    for copy in hy_copies:
        copy.start()
    for copy in hy_copies:
        copy.wait_recv()
    total = hy[...].astype(F32)
    for k in range(Y - 1):
        total = total + hy_r[k].astype(F32)
    hall[core, s, z] = total.astype(BF16)
    gz_copies = [
        rcopy(hall.at[core, s, z], hall.at[core, s, z], gz_send.at[k], gz_recv.at[k], z_peer(k))
        for k in range(1, Z)
    ]
    for copy in gz_copies:
        copy.start()

    for copy in z_copies:
        copy.wait_recv()
    total = cs32[pl.ds(pl.multiple_of(z * d.rz, d.rz), d.rz), :]
    for k in range(Z - 1):
        total = total + z_r[k].astype(F32)
    zsum[0 : d.rz, :] = total
    for k in range(X):
        part = zsum[k * d.rx : k * d.rx + d.rxp, :]
        xs32[k] = part
        xsb[k] = part.astype(BF16)
    x_copies = [
        rcopy(xsb.at[(s + k) % X], x_r.at[k - 1], x_send.at[k], x_recv.at[k], x_peer(k))
        for k in range(1, X)
    ]
    for copy in x_copies:
        copy.start()

    for k, copy in enumerate(gz_copies):
        sender = (z - k - 1 + Z) % Z
        rcopy(
            hall.at[core, s, sender], hall.at[core, s, sender], gz_send.at[k + 1],
            gz_recv.at[k + 1], z_peer(k + 1),
        ).wait_recv()
    gx_copies = [
        rcopy(hall.at[core, s], hall.at[core, s], gx_send.at[k], gx_recv.at[k], x_peer(k))
        for k in range(1, X)
    ]
    for copy in gx_copies:
        copy.start()

    for copy in x_copies:
        copy.wait_recv()
    total = xs32[s]
    for k in range(X - 1):
        total = total + x_r[k].astype(F32)
    hrow[pl.ds(0, d.rxp, stride=2), :] = total[:, 0:128]
    hrow[pl.ds(1, d.rxp, stride=2), :] = total[:, 128:256]
    for k in range(Y):
        ls[k] = hrow[k * d.hb : k * d.hb + d.hbp, :].astype(BF16)
    for k in range(Y):
        is_self = my_block == block0 + k
        copy = rcopy(ls.at[k], l_r.at[my_y], l_send.at[k], l_recv.at[my_y], owner(k))
        local = pltpu.make_async_copy(ls.at[k], l_r.at[my_y], l_recv.at[my_y])

        @pl.when(jnp.logical_not(is_self))
        def _():
            copy.start()

        @pl.when(is_self)
        def _():
            local.start()

    for k in range(1, X):
        sender = (s - k + X) % X
        rcopy(
            hall.at[core, sender], hall.at[core, sender], gx_send.at[k], gx_recv.at[k], x_peer(k)
        ).wait_recv()
    gcore = rcopy(hall.at[core], hall.at[core], core_send.at[2], core_recv.at[2], other_core)
    gcore.start()

    total = jnp.zeros((d.hbp, 128), F32)
    for k in range(Y):
        pltpu.make_async_copy(ls.at[k], l_r.at[k], l_recv.at[k]).wait()
    for k in range(Y):
        total = total + l_r[k].astype(F32)
    gconv_o[...] = total[0 : d.hb, :] * d.scale

    rcopy(
        hall.at[1 - core], hall.at[1 - core], core_send.at[2], core_recv.at[2], other_core
    ).wait_recv()
    for c in range(2):
        for x in range(X):
            for k in range(Z):
                at = c * d.hc + x * d.hx + k * d.hz
                h32[at : at + d.hz, :] = hall[c, x, k].astype(F32)[0 : d.hz, :]
    for half in range(d.head // C):
        gup_o[:, half * C : (half + 1) * C] = h32[half * C : (half + 1) * C, :] * d.scale
    for half in range(2):
        gout_o[half * depth : (half + 1) * depth, :] = (
            h32[base : base + depth, half * d.outc : (half + 1) * d.outc] * d.scale
        )

    def b_wait(step, _):
        sender = (me - step + N) % N
        rcopy(
            ret.at[sender], gcam_o.at[sender], b_send.at[step], b_recv.at[step], a_peer(step)
        ).wait_recv()
        return 0

    lax.fori_loop(1, N, b_wait, 0)

    def drain(step, _):
        a_copy(step).wait_send()
        b_copy(step).wait_send()
        return 0

    lax.fori_loop(1, N, drain, 0)
    for copy in (
        halo0 + halo1 + z_copies + x_copies + hx_copies + hz_copies + hy_copies
        + gz_copies + gx_copies + [core_copy, hcore_copy, gcore]
    ):
        copy.wait_send()
    for k in range(Y):
        copy = rcopy(ls.at[k], l_r.at[my_y], l_send.at[k], l_recv.at[my_y], owner(k))

        @pl.when(my_block != block0 + k)
        def _():
            copy.wait_send()

    maps_out.wait()
    gin_out.wait()
    own_out.wait()


def per_device(
    cam_send, lidar_bev, tile_active, tile_source, conv_weight, head_up, head_out, cotangent
):
    channels = cam_send.shape[5]
    cells_x, cells_y = lidar_bev.shape[1], lidar_bev.shape[2]
    head, outc = head_out.shape
    d = Dims(
        lax.axis_size("src"), lax.axis_size("gx"), lax.axis_size("gy"),
        cells_x, cells_y, channels, head, outc,
    )
    C, X, Y, Z, N = d.c, d.X, d.Y, d.Z, d.N
    cells = d.cells
    rows = tile_source.reshape(1, d.tiles)
    slots = jnp.arange(d.tiles, dtype=jnp.int32)
    inverse = jnp.sum(jnp.where(rows == slots[:, None], slots[None, :], 0), axis=1)

    vmem = pl.BlockSpec(memory_space=pltpu.VMEM)
    smem = pl.BlockSpec(memory_space=pltpu.SMEM)
    anyw = pl.BlockSpec(memory_space=pl.ANY)
    dma = pltpu.SemaphoreType.DMA

    def b16(*shape):
        return pltpu.VMEM(shape, BF16)

    def f32(*shape):
        return pltpu.VMEM(shape, F32)

    scratch = [
        b16(N, 2, 16, C), b16(cells, C), b16(3, 3 * C, C), b16(C, head), b16(head, outc),
        b16(cells, outc),
        b16(3, 3 * C, C), b16(head, C), b16(outc, head), f32(d.tx, cells_y, C),
        f32(cells_x, cells_y, C), b16((cells_x + 2) * cells_y, 3 * C), b16((cells_x + 2) * cells_y, 3 * C),
        b16(2, 2, cells_y, C), b16(2, 2, cells_y, C),
        b16(2, 2, d.colp, C), b16(2, 2, 3, d.colp, C),
        b16(cells, C), b16(cells, head), b16(cells, head), b16(cells, outc), b16(cells, C),
        b16(cells, C), b16(d.tiles, 16, C), b16(N, 2, 16, C),
        f32(d.rows, C), b16(d.rows, C), b16(d.rc, C), f32(d.rc, C),
        b16(Z, d.rz, C), b16(Z - 1, d.rz, C), f32(d.rz + 16, C),
        f32(X, d.rxp, C), b16(X, d.rxp, C), b16(X - 1, d.rxp, C),
        f32(2 * d.rxp + 16, 128), b16(Y, d.hbp, 128), b16(Y, d.hbp, 128),
        f32(d.hrows, C), b16(d.hrows, C), b16(d.hc, C), f32(d.hc, C),
        b16(X, d.hx, C), b16(X - 1, d.hx, C), f32(d.hx + 16, C),
        f32(Z, d.hzp, C), b16(Z, d.hzp, C), b16(Z - 1, d.hzp, C),
        b16(d.hzp, C), b16(Y - 1, d.hzp, C), b16(2, X, Z, d.hzp, C),
        dma((6,)), dma((3,)),
        dma((N,)), dma((N,)), dma((N,)), dma((N,)),
        dma((2, 8)), dma((2, 8)), dma((3,)), dma((3,)),
        dma((Z,)), dma((Z,)), dma((X,)), dma((X,)), dma((Y,)), dma((Y,)),
        dma((X,)), dma((X,)), dma((Z,)), dma((Z,)), dma((Y,)), dma((Y,)),
        dma((Z,)), dma((Z,)), dma((X,)), dma((X,)),
    ]
    maps, gin, gcam, gconv, gup, gout = pl.pallas_call(
        functools.partial(kernel, d),
        out_shape=(
            jax.ShapeDtypeStruct((cells, outc), BF16),
            jax.ShapeDtypeStruct((cells, C), BF16),
            jax.ShapeDtypeStruct((N, 2, 16, C), BF16),
            jax.ShapeDtypeStruct((d.hb, 128), F32),
            jax.ShapeDtypeStruct((C, head), F32),
            jax.ShapeDtypeStruct((head, outc), F32),
        ),
        in_specs=[anyw, anyw, vmem, smem, smem, anyw, anyw, anyw, anyw],
        out_specs=(anyw, anyw, anyw, vmem, vmem, vmem),
        scratch_shapes=scratch,
        compiler_params=pltpu.CompilerParams(
            collective_id=0, has_side_effects=True, vmem_limit_bytes=48 * 1024 * 1024
        ),
    )(
        cam_send.reshape(N, 2, 16, C),
        lidar_bev.reshape(cells, C),
        tile_active.reshape(d.tx, d.ty),
        tile_source.reshape(d.tx, d.ty),
        inverse,
        conv_weight.reshape(3, 3 * C, C),
        head_up,
        head_out,
        cotangent.reshape(cells, outc),
    )
    return (
        maps.reshape(1, cells_x, cells_y, outc),
        gin.reshape(1, cells_x, cells_y, C),
        gcam.reshape(1, 1, N, 2, 16, C),
        gconv.reshape(-1),
        gup,
        gout,
    )


def solution(mesh):
    in_specs = (
        P(("src", "gx"), "gy", None, None, None, None),
        P("src", "gx", "gy", None),
        P("src", "gx", "gy"),
        P("src", "gx", "gy"),
        P(),
        P(),
        P(),
        P("src", "gx", "gy", None),
    )
    out_specs = (
        P("src", "gx", "gy", None),
        P("src", "gx", "gy", None),
        P(("src", "gx"), "gy", None, None, None, None),
        P(("src", "gx", "gy")),
        P(),
        P(),
    )
    return jax.shard_map(
        per_device, mesh=mesh, in_specs=in_specs, out_specs=out_specs, check_vma=False
    )
```

```python
import functools
import math

import jax
import jax.numpy as jnp
from jax import lax
from jax.experimental import pallas as pl
from jax.experimental.pallas import tpu as pltpu
from jax.sharding import PartitionSpec as P

MESH = pl.DeviceIdType.MESH
F32 = jnp.float32
BF16 = jnp.bfloat16


def pad16(rows):
    return (rows + 15) // 16 * 16


def sigmoid(value):
    return 0.5 * jnp.tanh(0.5 * value) + 0.5


def dot(lhs, rhs):
    return jnp.dot(lhs, rhs, preferred_element_type=F32)


def dot_tn(lhs, rhs):
    return lax.dot_general(lhs, rhs, (((0,), (0,)), ((), ())), preferred_element_type=F32)


def rcopy(src, dst, send_sem, recv_sem, device):
    return pltpu.make_async_remote_copy(
        src_ref=src,
        dst_ref=dst,
        send_sem=send_sem,
        recv_sem=recv_sem,
        device_id=device,
        device_id_type=MESH,
    )


class Dims:
    def __init__(self, n_src, n_gx, n_gy, cells_x, cells_y, channels, head, outc):
        self.X, self.GX, self.GY = n_src, n_gx, n_gy
        self.YL, self.Z, self.Y = n_gx // 2, n_gy // 2, n_gx
        self.N = n_src * n_gx
        self.cx, self.cy, self.c = cells_x, cells_y, channels
        self.cells = cells_x * cells_y
        self.tx, self.ty = cells_x // 4, cells_y // 4
        self.tiles = self.tx * self.ty
        self.head, self.outc = head, outc
        self.colp = pad16(cells_x)
        self.rows = 9 * channels
        self.rc = self.rows // 2
        self.ra = self.rc // 2
        self.az = self.ra // self.Z
        self.azp = pad16(self.az)
        self.bx = self.ra // self.X
        self.rl = self.az // self.X
        self.rlp = pad16(self.rl)
        self.nb = self.Y // 2
        self.hb = 2 * self.rl // self.nb
        self.hbp = pad16(self.hb)
        self.hrows = (channels * head + head * outc) // channels
        self.hc = self.hrows // 2
        self.hx = self.hc // self.X
        self.hz = self.hx // self.Z
        self.hzp = pad16(self.hz)
        self.scale = 1.0 / math.sqrt(n_src * n_gx * n_gy * cells_x * cells_y)


def kernel(
    d,
    cam, lidar_h, act_h, tsrc_h, wconv_h, hup_h, hout_h, cot_h,
    maps_o, gin_o, gcam_o, gconv_o, gup_o, gout_o,
    arrived, lidar, wconv, hup, hout, cot, act, tvec, tsrc, inv_v, inv,
    wt, hup_t, hout_t, mask,
    m32, m3, g3, rows_s, rows_r, cols_s, cols_r,
    feat, hid, gh, maps, gp, gi, tiles, ret,
    dw32, dwb, core_r, cs32,
    az, az_r, azsum, ax32, ax, ax_r, ahrow,
    bx, bx_r, bxsum, bz32, bz, bz_r, bhrow, ls, l_r,
    h32, hb, hcore_r, hs32, hxs, hx_r, hxsum, hzs32, hzs, hz_r, hy, hy_r, hpart, hpack, hall,
    in_sem, out_sem,
    a_send, a_recv, b_send, b_recv, row_send, row_recv, col_send, col_recv, core_send, core_recv,
    az_send, az_recv, ax_send, ax_recv, bx_send, bx_recv, bz_send, bz_recv, l_send, l_recv,
    hx_send, hx_recv, hz_send, hz_recv, hy_send, hy_recv, gz_send, gz_recv, gx_send, gx_recv,
):
    s = lax.axis_index("src")
    g = lax.axis_index("gx")
    r = lax.axis_index("gy")
    core, yl = g % 2, g // 2
    z, yh = r // 2, r % 2
    me = s * d.GX + g
    X, Y, Z, N, C, CY = d.X, d.Y, d.Z, d.N, d.c, d.cy

    loads = [
        pltpu.make_async_copy(src, dst, in_sem.at[k])
        for k, (src, dst) in enumerate(
            [(act_h, act), (tsrc_h, tvec), (tsrc_h, tsrc), (wconv_h, wconv), (hup_h, hup),
             (hout_h, hout), (lidar_h, lidar), (cot_h, cot), (cam.at[me], arrived.at[me])]
        )
    ]

    order = {1: (0,), 2: (1, 0)}.get(d.YL) or (d.YL // 2, *[k for k in range(1, d.YL) if k != d.YL // 2], 0)

    def a_peer(far, step):
        to_s = (s + step // 2) % X
        to_g = ((yl + far) % d.YL) * 2 + (core + step) % 2
        return to_s * d.GX + to_g, (to_s, to_g, r)

    def each_peer(body):
        for far in order:
            lax.fori_loop(0 if far else 1, 2 * X, lambda step, _, far=far: body(far, step) or 0, 0)

    def z_peer(step):
        return (s, g, ((z + step) % Z) * 2 + yh)

    def x_peer(step):
        return ((s + step) % X, g, r)

    def y_peer(step):
        at = (yl * 2 + yh + step) % Y
        return (s, (at // 2) * 2 + core, z * 2 + at % 2)

    other_core = (s, yl * 2 + 1 - core, r)

    my_block = (s * d.GX + g) * d.GY + r
    per_half = Z * X * d.nb
    from_core = my_block // (2 * per_half)
    from_b = (my_block // per_half) % 2
    place = (my_block % per_half) // d.nb
    from_z = jnp.where(from_b == 1, place % Z, place // X)
    from_x = jnp.where(from_b == 1, place // Z, place % X)
    my_y = yl * 2 + yh

    def block_of(half, k):
        where = z * X + s if half == 0 else s * Z + z
        return (core * 2 + half) * per_half + where * d.nb + k

    def owner(block):
        return (block // (d.GX * d.GY), (block // d.GY) % d.GX, block % d.GY)

    def last_sender(at):
        return (from_x, (at // 2) * 2 + from_core, from_z * 2 + at % 2)

    self_group = jnp.logical_and(
        jnp.logical_and(from_core == core, from_z == z), from_x == s
    )

    barrier = pltpu.get_barrier_semaphore()

    def greet(device):
        pl.semaphore_signal(barrier, inc=1, device_id=device, device_id_type=MESH)

    each_peer(lambda far, step: greet(a_peer(far, step)[1]))
    count = N - 1
    for step in range(1, Z):
        greet(z_peer(step))
        count += 1
    for at in range(d.YL):
        greet((s, at * 2 + core, z * 2 + 1 - yh))
        count += 1
    for side in (-1, 1):
        for near in (-1, 0, 1):
            greet((s, (g + near + d.GX) % d.GX, (r + side + d.GY) % d.GY))
            count += 1
    for at in range(Y):
        is_self = jnp.logical_and(self_group, my_y == at)

        @pl.when(jnp.logical_not(is_self))
        def _():
            greet(last_sender(at))

    count = count + Y - jnp.where(self_group, 1, 0)
    pl.semaphore_wait(barrier, count)

    def a_start(far, step):
        to, device = a_peer(far, step)
        rcopy(cam.at[to], arrived.at[me], a_send, a_recv, device).start()

    each_peer(a_start)
    for load in loads:
        load.start()

    for load in loads[:6]:
        load.wait()
    at_y = lax.broadcasted_iota(jnp.int32, (CY, d.ty), 0) // 4
    at_q = lax.broadcasted_iota(jnp.int32, (CY, d.ty), 1)
    for p in range(d.tx):
        row = act[p : p + 1, :].astype(F32)
        column = jnp.sum(jnp.where(at_y == at_q, row, 0.0), axis=1, keepdims=True)
        mask[p] = jnp.broadcast_to(column, (CY, C))
    eye = lax.broadcasted_iota(jnp.int32, (d.ty, d.ty), 0) == lax.broadcasted_iota(
        jnp.int32, (d.ty, d.ty), 1
    )
    at_t = lax.broadcasted_iota(jnp.int32, (d.ty, 128), 0)
    at_s = lax.broadcasted_iota(jnp.int32, (d.ty, 128), 1)
    found = jnp.zeros((1, 128), jnp.int32)
    for p in range(d.tx):
        column = jnp.sum(jnp.where(eye, tvec[p : p + 1, :], 0), axis=1, keepdims=True)
        hit = jnp.where(column == at_s, at_t + p * d.ty, 0)
        found = jnp.maximum(found, jnp.max(hit, axis=0, keepdims=True))
    inv_v[...] = jnp.broadcast_to(found, (8, 128))
    inv_copy = pltpu.make_async_copy(inv_v, inv, in_sem.at[0])
    inv_copy.start()
    for i in range(3):
        for j in range(3):
            tap = wconv[2 - i, (2 - j) * C : (3 - j) * C, :].astype(F32)
            wt[i, j * C : (j + 1) * C, :] = tap.T.astype(BF16)
    hup_t[...] = hup[...].astype(F32).T.astype(BF16)
    hout_t[...] = hout[...].astype(F32).T.astype(BF16)

    inv_copy.wait()
    for load in loads[6:]:
        load.wait()
    all_but_one = pl.ds(0, N - 1)
    rcopy(
        arrived.at[all_but_one], arrived.at[all_but_one], a_send, a_recv, other_core
    ).wait_recv()

    span = 4 * CY

    def merge(p, _):
        for q in range(d.ty):
            at = tsrc[p, q]
            tile = arrived[at // 2, at % 2].astype(F32)
            for dx in range(4):
                m32[4 * p + dx, 4 * q : 4 * q + 4, :] = tile[4 * dx : 4 * dx + 4]
        for dx in range(4):
            x = 4 * p + dx
            line = pl.ds(pl.multiple_of(x * CY, CY), CY)
            m32[x] = mask[p] * (m32[x] + lidar[line, :].astype(F32))
        return 0

    lax.fori_loop(0, d.tx, merge, 0)

    def send_all(parts, slots, size, here, peer, send_sem, recv_sem):
        for k in range(1, size):
            rcopy(parts.at[(here + k) % size], slots.at[k - 1], send_sem, recv_sem, peer(k)).start()
        return rcopy(slots, slots, send_sem, recv_sem, other_core)

    def halo_start(k):
        rows_s[k, 0] = m32[0].astype(BF16)
        rows_s[k, 1] = m32[d.cx - 1].astype(BF16)
        cols_s[k, 0, 0 : d.cx, :] = m32[:, 0, :].astype(BF16)
        cols_s[k, 1, 0 : d.cx, :] = m32[:, CY - 1, :].astype(BF16)
        for side, step in ((0, -1), (1, 1)):
            for near in (-1, 0, 1):
                device = (s, (g + near + d.GX) % d.GX, (r + step + d.GY) % d.GY)
                rcopy(
                    cols_s.at[k, side], cols_r.at[k, 1 - side, 1 - near], col_send.at[k],
                    col_recv.at[k], device,
                ).start()
            device = (s, (g + step + d.GX) % d.GX, r)
            rcopy(
                rows_s.at[k, side], rows_r.at[k, 1 - side], row_send.at[k], row_recv.at[k], device
            ).start()

    at_row = lax.broadcasted_iota(jnp.int32, (CY, C), 0)
    head_row = lax.broadcasted_iota(jnp.int32, (16, C), 0)

    def put(out3, x, line, left, right):
        down = jnp.where(at_row == 0, left, pltpu.roll(line, 1, 0))
        up = jnp.where(at_row == CY - 1, right, pltpu.roll(line, CY - 1, 0))
        out3[x * CY : (x + 1) * CY, 0:C] = down.astype(BF16)
        out3[x * CY : (x + 1) * CY, C : 2 * C] = line.astype(BF16)
        out3[x * CY : (x + 1) * CY, 2 * C : 3 * C] = up.astype(BF16)

    def put_ends(out3, x, left, right):
        top = m32[x - 1, 0:16, :]
        low = m32[x - 1, CY - 16 : CY, :]
        down = jnp.where(head_row == 0, left, pltpu.roll(top, 1, 0))
        up = jnp.where(head_row == 15, right, pltpu.roll(low, 15, 0))
        out3[x * CY : x * CY + 16, 0:C] = down.astype(BF16)
        out3[(x + 1) * CY - 16 : (x + 1) * CY, 2 * C : 3 * C] = up.astype(BF16)

    def halo_inner(out3):
        for x in range(d.cx):
            put(out3, x + 1, m32[x], 0.0, 0.0)

    def halo_finish(k, out3, ends):
        rcopy(rows_s.at[k], rows_r.at[k], row_send.at[k], row_recv.at[k], other_core).wait_recv()
        rcopy(cols_r.at[k], cols_r.at[k], col_send.at[k], col_recv.at[k], other_core).wait_recv()
        ok_g = (g > 0, g < d.GX - 1)
        ok_r = (r > 0, r < d.GY - 1)
        lefts = [jnp.where(ok_r[0], cols_r[k, 0, near].astype(F32), 0.0) for near in range(3)]
        rights = [jnp.where(ok_r[1], cols_r[k, 1, near].astype(F32), 0.0) for near in range(3)]
        for side, x, row in ((0, 0, d.cx - 1), (1, d.cx + 1, 0)):
            line = rows_r[k, side].astype(F32)
            near = 0 if side == 0 else 2
            line, left, right = [
                jnp.where(ok_g[side], value, 0.0)
                for value in (line, lefts[near][row : row + 1], rights[near][row : row + 1])
            ]
            put(out3, x, line, left, right)
        for x in range(d.cx):
            left, right = lefts[1][x : x + 1], rights[1][x : x + 1]
            if ends:
                put_ends(out3, x + 1, left, right)
            else:
                put(out3, x + 1, m32[x], left, right)

    halo_start(0)
    halo_inner(m3)
    halo_finish(0, m3, True)

    def forward(p, _):
        here = pl.ds(pl.multiple_of(p * span, span), span)
        pre = jnp.zeros((span, C), F32)
        for i in range(3):
            pre = pre + dot(
                m3[pl.ds(pl.multiple_of(p * span + i * CY, CY), span), :], wconv[i]
            )
        occupied = jnp.concatenate([mask[p]] * 4, axis=0)
        sig = sigmoid(pre)
        feature = (occupied * (pre * sig)).astype(BF16)
        slope = occupied * (sig * (1.0 + pre * (1.0 - sig)))
        feat[here, :] = feature
        lines = pl.ds(4 * p, 4)
        m32[lines] = slope.reshape(4, CY, C)
        up = dot(feature, hup[...])
        sig = sigmoid(up)
        hidden = (up * sig).astype(BF16)
        hid[here, :] = hidden
        maps[here, :] = dot(hidden, hout[...]).astype(BF16)
        grad = (dot(cot[here, :], hout_t[...]) * (sig * (1.0 + up * (1.0 - sig)))).astype(BF16)
        gh[here, :] = grad
        value = dot(grad, hup_t[...]) * m32[lines].reshape(span, C)
        m32[lines] = value.reshape(4, CY, C)
        gp[here, :] = value.astype(BF16)
        return 0

    lax.fori_loop(0, d.tx, forward, 0)
    halo_start(1)
    maps_out = pltpu.make_async_copy(maps, maps_o, out_sem.at[0])
    maps_out.start()

    def last(half, total, rows):
        rows[pl.ds(0, d.rlp, stride=2), :] = total[:, 0:128]
        rows[pl.ds(1, d.rlp, stride=2), :] = total[:, 128:256]
        for k in range(d.nb):
            at = half * d.nb + k
            ls[at] = rows[k * d.hb : k * d.hb + d.hbp, :].astype(BF16)
            block = block_of(half, k)
            copy = rcopy(ls.at[at], l_r.at[my_y], l_send, l_recv, owner(block))
            local = pltpu.make_async_copy(ls.at[at], l_r.at[my_y], l_recv)

            @pl.when(block != my_block)
            def _():
                copy.start()

            @pl.when(block == my_block)
            def _():
                local.start()

    term = dot_tn(feat[...], gh[...])
    for half in range(d.head // C):
        h32[half * C : (half + 1) * C, :] = term[:, half * C : (half + 1) * C]
    base = d.head
    term = dot_tn(hid[...], cot[...])
    depth = d.head // 2
    for half in range(2):
        h32[base : base + depth, half * d.outc : (half + 1) * d.outc] = term[
            half * depth : (half + 1) * depth, :
        ]
    hb[...] = h32[...].astype(BF16)
    hmine = pl.ds(pl.multiple_of(core * d.hc, d.hc), d.hc)
    htheirs = pl.ds(pl.multiple_of((1 - core) * d.hc, d.hc), d.hc)
    hcore_copy = rcopy(hb.at[htheirs], hcore_r, core_send.at[1], core_recv.at[1], other_core)
    hcore_copy.start()

    def tap_grads(i, _):
        for j in range(3):
            term = dot_tn(
                m3[pl.ds(pl.multiple_of(i * CY, CY), d.cells), j * C : (j + 1) * C], gp[...]
            )
            at = pl.ds(pl.multiple_of(i * (3 * C) + j * C, C), C)
            dw32[at, :] = term
            dwb[at, :] = term.astype(BF16)
        return 0

    lax.fori_loop(0, 3, tap_grads, 0)
    mine = pl.ds(pl.multiple_of(core * d.rc, d.rc), d.rc)
    theirs = pl.ds(pl.multiple_of((1 - core) * d.rc, d.rc), d.rc)
    core_copy = rcopy(dwb.at[theirs], core_r, core_send.at[0], core_recv.at[0], other_core)
    core_copy.start()

    hcore_copy.wait_recv()
    hs32[...] = h32[hmine, :] + hcore_r[...].astype(F32)
    for k in range(X):
        hxs[k] = hs32[k * d.hx : (k + 1) * d.hx, :].astype(BF16)
    hx_wait = send_all(hxs, hx_r, X, s, x_peer, hx_send, hx_recv)

    halo_finish(1, g3, False)

    hx_wait.wait_recv()
    total = hs32[pl.ds(pl.multiple_of(s * d.hx, d.hx), d.hx), :]
    for k in range(X - 1):
        total = total + hx_r[k].astype(F32)
    hxsum[0 : d.hx, :] = total
    for k in range(Z):
        part = hxsum[k * d.hz : k * d.hz + d.hzp, :]
        hzs32[k] = part
        hzs[k] = part.astype(BF16)
    hz_wait = send_all(hzs, hz_r, Z, z, z_peer, hz_send, hz_recv)

    core_copy.wait_recv()
    cs32[...] = dw32[mine, :] + core_r[...].astype(F32)
    for k in range(Z):
        az[k] = cs32[k * d.az : k * d.az + d.azp, :].astype(BF16)
    az_wait = send_all(az, az_r, Z, z, z_peer, az_send, az_recv)
    for k in range(X):
        bx[k] = cs32[d.ra + k * d.bx : d.ra + (k + 1) * d.bx, :].astype(BF16)
    bx_wait = send_all(bx, bx_r, X, s, x_peer, bx_send, bx_recv)

    def backward(p, _):
        here = pl.ds(pl.multiple_of(p * span, span), span)
        acc = jnp.zeros((span, C), F32)
        for i in range(3):
            acc = acc + dot(g3[pl.ds(pl.multiple_of(p * span + i * CY, CY), span), :], wt[i])
        acc = acc * jnp.concatenate([mask[p]] * 4, axis=0)
        gi[here, :] = acc.astype(BF16)
        m32[pl.ds(4 * p, 4)] = acc.reshape(4, CY, C)
        for q in range(d.ty):
            parts = [m32[4 * p + dx, 4 * q : 4 * q + 4, :] for dx in range(4)]
            tiles[p * d.ty + q] = jnp.concatenate(parts, axis=0).astype(BF16)
        return 0

    lax.fori_loop(0, d.tx, backward, 0)
    gin_out = pltpu.make_async_copy(gi, gin_o, out_sem.at[1])
    gin_out.start()

    hz_wait.wait_recv()
    total = hzs32[z]
    for k in range(Z - 1):
        total = total + hz_r[k].astype(F32)
    hy[...] = total.astype(BF16)
    for k in range(1, Y):
        rcopy(hy, hy_r.at[k - 1], hy_send, hy_recv, y_peer(k)).start()
    hy_wait = rcopy(hy_r, hy_r, hy_send, hy_recv, other_core)

    def b_start(far, step):
        to, device = a_peer(far, step)
        for slot in range(2):
            ret[to, slot] = tiles[inv[0, to * 2 + slot]]
        rcopy(ret.at[to], gcam_o.at[me], b_send, b_recv, device).start()

    each_peer(b_start)
    for slot in range(2):
        ret[me, slot] = tiles[inv[0, me * 2 + slot]]
    own_out = pltpu.make_async_copy(ret.at[me], gcam_o.at[me], out_sem.at[2])
    own_out.start()

    bx_wait.wait_recv()
    total = cs32[pl.ds(pl.multiple_of(d.ra + s * d.bx, 8), d.bx), :]
    for k in range(X - 1):
        total = total + bx_r[k].astype(F32)
    bxsum[0 : d.bx, :] = total
    for k in range(Z):
        part = bxsum[k * d.rl : k * d.rl + d.rlp, :]
        bz32[k] = part
        bz[k] = part.astype(BF16)
    bz_wait = send_all(bz, bz_r, Z, z, z_peer, bz_send, bz_recv)

    hy_wait.wait_recv()
    total = hy[...].astype(F32)
    for k in range(Y - 1):
        total = total + hy_r[k].astype(F32)
    hpart[z] = total.astype(BF16)
    part = hpart.at[z]
    for k in range(1, Z):
        rcopy(part, part, gz_send, gz_recv, z_peer(k)).start()

    az_wait.wait_recv()
    total = cs32[pl.ds(pl.multiple_of(z * d.az, 8), d.azp), :]
    for k in range(Z - 1):
        total = total + az_r[k].astype(F32)
    azsum[0 : d.azp, :] = total
    for k in range(X):
        part = azsum[k * d.rl : k * d.rl + d.rlp, :]
        ax32[k] = part
        ax[k] = part.astype(BF16)
    ax_wait = send_all(ax, ax_r, X, s, x_peer, ax_send, ax_recv)

    parts = hpart.at[pl.ds(0, Z - 1)]
    gz_wait = rcopy(parts, parts, gz_send, gz_recv, other_core)
    gz_wait.wait_recv()
    for k in range(Z):
        hpack[k * d.hz : k * d.hz + d.hzp, :] = hpart[k].astype(F32)
    hall[core, s] = hpack[0 : d.hx, :].astype(BF16)
    part = hall.at[core, s]
    for k in range(1, X):
        rcopy(part, part, gx_send, gx_recv, x_peer(k)).start()

    bz_wait.wait_recv()
    total = bz32[z]
    for k in range(Z - 1):
        total = total + bz_r[k].astype(F32)
    last(1, total, bhrow)
    ax_wait.wait_recv()
    total = ax32[s]
    for k in range(X - 1):
        total = total + ax_r[k].astype(F32)
    last(0, total, ahrow)

    parts = hall.at[core, pl.ds(0, X - 1)]
    gx_wait = rcopy(parts, parts, gx_send, gx_recv, other_core)
    gx_wait.wait_recv()
    gcore = rcopy(hall.at[core], hall.at[core], core_send.at[2], core_recv.at[2], other_core)
    gcore.start()

    total = jnp.zeros((d.hbp, 128), F32)
    pltpu.make_async_copy(ls, l_r, l_recv).wait()
    for k in range(Y):
        total = total + l_r[k].astype(F32)
    gconv_o[...] = total[0 : d.hb, :] * d.scale

    rcopy(
        hall.at[1 - core], hall.at[1 - core], core_send.at[2], core_recv.at[2], other_core
    ).wait_recv()
    for c in range(2):
        for x in range(X):
            at = c * d.hc + x * d.hx
            h32[at : at + d.hx, :] = hall[c, x].astype(F32)
    for half in range(d.head // C):
        gup_o[:, half * C : (half + 1) * C] = h32[half * C : (half + 1) * C, :] * d.scale
    for half in range(2):
        gout_o[half * depth : (half + 1) * depth, :] = (
            h32[base : base + depth, half * d.outc : (half + 1) * d.outc] * d.scale
        )

    parts = ret.at[all_but_one]
    b_wait = rcopy(parts, gcam_o.at[all_but_one], b_send, b_recv, other_core)
    b_wait.wait_recv()

    rcopy(parts, parts, a_send, a_recv, other_core).wait_send()
    b_wait.wait_send()
    for k in range(2):
        rcopy(rows_s.at[k], rows_r.at[k], row_send.at[k], row_recv.at[k], other_core).wait_send()
        rcopy(cols_r.at[k], cols_r.at[k], col_send.at[k], col_recv.at[k], other_core).wait_send()
    for wait in (
        az_wait, ax_wait, bx_wait, bz_wait, hx_wait, hz_wait, hy_wait, gz_wait, gx_wait,
        core_copy, hcore_copy, gcore,
    ):
        wait.wait_send()

    @pl.when(self_group)
    def _():
        parts = ls.at[pl.ds(0, Y - 1)]
        rcopy(parts, parts, l_send, l_recv, other_core).wait_send()

    @pl.when(jnp.logical_not(self_group))
    def _():
        rcopy(ls, ls, l_send, l_recv, other_core).wait_send()

    maps_out.wait()
    gin_out.wait()
    own_out.wait()


def copy_kernel(*refs):
    loads = [
        pltpu.make_async_copy(refs[k], refs[12 + k], refs[18].at[k]) for k in range(6)
    ]
    stores = [
        pltpu.make_async_copy(refs[12 + k], refs[6 + k], refs[18].at[k]) for k in range(6)
    ]
    for load in loads:
        load.start()
    for load, store in zip(loads, stores):
        load.wait()
        store.start()
    for store in stores:
        store.wait()


def per_device(
    cam_send, lidar_bev, tile_active, tile_source, conv_weight, head_up, head_out, cotangent
):
    channels = cam_send.shape[5]
    cells_x, cells_y = lidar_bev.shape[1], lidar_bev.shape[2]
    head, outc = head_out.shape
    d = Dims(
        lax.axis_size("src"), lax.axis_size("gx"), lax.axis_size("gy"),
        cells_x, cells_y, channels, head, outc,
    )
    C, X, Y, Z, N = d.c, d.X, d.Y, d.Z, d.N
    cells = d.cells
    vmem = pl.BlockSpec(memory_space=pltpu.VMEM)
    anyw = pl.BlockSpec(memory_space=pl.ANY)
    dma = pltpu.SemaphoreType.DMA

    def b16(*shape):
        return pltpu.VMEM(shape, BF16)

    def f32(*shape):
        return pltpu.VMEM(shape, F32)

    def i32(*shape):
        return pltpu.VMEM(shape, jnp.int32)

    scratch = [
        b16(N, 2, 16, C), b16(cells, C), b16(3, 3 * C, C), b16(C, head), b16(head, outc),
        b16(cells, outc), i32(d.tx, d.ty), i32(d.tx, d.ty), pltpu.SMEM((d.tx, d.ty), jnp.int32),
        i32(8, 128), pltpu.SMEM((8, 128), jnp.int32),
        b16(3, 3 * C, C), b16(head, C), b16(outc, head), f32(d.tx, cells_y, C),
        f32(cells_x, cells_y, C), b16((cells_x + 2) * cells_y, 3 * C), b16((cells_x + 2) * cells_y, 3 * C),
        b16(2, 2, cells_y, C), b16(2, 2, cells_y, C),
        b16(2, 2, d.colp, C), b16(2, 2, 3, d.colp, C),
        b16(cells, C), b16(cells, head), b16(cells, head), b16(cells, outc), b16(cells, C),
        b16(cells, C), b16(d.tiles, 16, C), b16(N, 2, 16, C),
        f32(d.rows, C), b16(d.rows, C), b16(d.rc, C), f32(d.rc, C),
        b16(Z, d.azp, C), b16(Z - 1, d.azp, C), f32(d.azp + d.rlp, C),
        f32(X, d.rlp, C), b16(X, d.rlp, C), b16(X - 1, d.rlp, C), f32(2 * d.rlp, 128),
        b16(X, d.bx, C), b16(X - 1, d.bx, C), f32(d.bx + d.rlp, C),
        f32(Z, d.rlp, C), b16(Z, d.rlp, C), b16(Z - 1, d.rlp, C), f32(2 * d.rlp, 128),
        b16(Y, d.hbp, 128), b16(Y, d.hbp, 128),
        f32(d.hrows, C), b16(d.hrows, C), b16(d.hc, C), f32(d.hc, C),
        b16(X, d.hx, C), b16(X - 1, d.hx, C), f32(d.hx + 16, C),
        f32(Z, d.hzp, C), b16(Z, d.hzp, C), b16(Z - 1, d.hzp, C),
        b16(d.hzp, C), b16(Y - 1, d.hzp, C),
        b16(Z, d.hzp, C), f32(d.hx + 16, C), b16(2, X, d.hx, C),
        dma((9,)), dma((3,)),
        dma, dma, dma, dma, dma((2,)), dma((2,)), dma((2,)), dma((2,)), dma((3,)), dma((3,)),
        *[dma] * 20,
    ]
    results = pl.pallas_call(
        functools.partial(kernel, d),
        out_shape=(
            jax.ShapeDtypeStruct((cells, outc), BF16),
            jax.ShapeDtypeStruct((cells, C), BF16),
            jax.ShapeDtypeStruct((N, 2, 16, C), BF16),
            jax.ShapeDtypeStruct((d.hb, 128), F32),
            jax.ShapeDtypeStruct((C, head), F32),
            jax.ShapeDtypeStruct((head, outc), F32),
        ),
        in_specs=[anyw] * 8,
        out_specs=(anyw, anyw, anyw, vmem, vmem, vmem),
        scratch_shapes=scratch,
        compiler_params=pltpu.CompilerParams(
            collective_id=0, has_side_effects=True, vmem_limit_bytes=64 * 1024 * 1024
        ),
    )(
        cam_send.reshape(N, 2, 16, C),
        lidar_bev.reshape(cells, C),
        tile_active.reshape(d.tx, d.ty),
        tile_source.reshape(d.tx, d.ty),
        conv_weight.reshape(3, 3 * C, C),
        head_up,
        head_out,
        cotangent.reshape(cells, outc),
    )
    maps, gin, gcam, gconv, gup, gout = pl.pallas_call(
        copy_kernel,
        out_shape=tuple(jax.ShapeDtypeStruct(a.shape, a.dtype) for a in results),
        in_specs=[anyw] * 6,
        out_specs=(anyw,) * 6,
        scratch_shapes=[*[pltpu.VMEM(a.shape, a.dtype) for a in results], dma((6,))],
        compiler_params=pltpu.CompilerParams(vmem_limit_bytes=64 * 1024 * 1024),
    )(*results)
    return (
        maps.reshape(1, cells_x, cells_y, outc),
        gin.reshape(1, cells_x, cells_y, C),
        gcam.reshape(1, 1, N, 2, 16, C),
        gconv.reshape(-1),
        gup,
        gout,
    )


def solution(mesh):
    in_specs = (
        P(("src", "gx"), "gy", None, None, None, None),
        P("src", "gx", "gy", None),
        P("src", "gx", "gy"),
        P("src", "gx", "gy"),
        P(),
        P(),
        P(),
        P("src", "gx", "gy", None),
    )
    out_specs = (
        P("src", "gx", "gy", None),
        P("src", "gx", "gy", None),
        P(("src", "gx"), "gy", None, None, None, None),
        P(("src", "gx", "gy")),
        P(),
        P(),
    )
    return jax.shard_map(
        per_device, mesh=mesh, in_specs=in_specs, out_specs=out_specs, check_vma=False
    )
```

```python
import functools
import math

import jax
import jax.numpy as jnp
from jax import lax
from jax.experimental import pallas as pl
from jax.experimental.pallas import tpu as pltpu
from jax.sharding import PartitionSpec as P

MESH = pl.DeviceIdType.MESH
F32 = jnp.float32
BF16 = jnp.bfloat16


def pad16(rows):
    return (rows + 15) // 16 * 16


def sigmoid(value):
    return 0.5 * jnp.tanh(0.5 * value) + 0.5


def dot(lhs, rhs):
    return jnp.dot(lhs, rhs, preferred_element_type=F32)


def dot_tn(lhs, rhs):
    return lax.dot_general(lhs, rhs, (((0,), (0,)), ((), ())), preferred_element_type=F32)


def rcopy(src, dst, send_sem, recv_sem, device):
    return pltpu.make_async_remote_copy(
        src_ref=src,
        dst_ref=dst,
        send_sem=send_sem,
        recv_sem=recv_sem,
        device_id=device,
        device_id_type=MESH,
    )


class Dims:
    def __init__(self, n_src, n_gx, n_gy, cells_x, cells_y, channels, head, outc):
        self.X, self.GX, self.GY = n_src, n_gx, n_gy
        self.YL, self.Z, self.Y = n_gx // 2, n_gy // 2, n_gx
        self.N = n_src * n_gx
        self.cx, self.cy, self.c = cells_x, cells_y, channels
        self.cells = cells_x * cells_y
        self.tx, self.ty = cells_x // 4, cells_y // 4
        self.tiles = self.tx * self.ty
        self.head, self.outc = head, outc
        self.colp = pad16(cells_x)
        self.rows = 9 * channels
        self.rc = self.rows // 2
        self.bx = self.rc // self.X
        self.rl = self.bx // self.Z
        self.rlp = pad16(self.rl)
        self.hb = 2 * self.rl // self.Y
        self.hbp = pad16(self.hb)
        self.hrows = (channels * head + head * outc) // channels
        self.hc = self.hrows // 2
        self.hx = self.hc // self.X
        self.hz = self.hx // self.Z
        self.hzp = pad16(self.hz)
        self.scale = 1.0 / math.sqrt(n_src * n_gx * n_gy * cells_x * cells_y)


def kernel(
    d,
    cam, lidar_h, act_h, tsrc_h, wconv_h, hup_h, hout_h, cot_h,
    maps_o, gin_o, gcam_o, gconv_o, gup_o, gout_o,
    arrived, lidar, wconv, hup, hout, cot, act, tvec, tsrc, inv_v, inv,
    wt, hup_t, hout_t, mask,
    m32, conv, m3, g3, rows_s, rows_r, cols_s, cols_r,
    feat, hid, gh, maps, gp, gi, tiles, ret,
    dw32, dwb, core_r, cs32,
    bx, bx_r, bxsum, bz32, bz, bz_r, brow, ls, l_r,
    h32, hb, hcore_r, hs32, hxs, hx_r, hxsum, hzs32, hzs, hz_r, hy, hy_r, hpart, hpack, hall,
    in_sem, out_sem,
    a_send, a_recv, b_send, b_recv, row_send, row_recv, col_send, col_recv, core_send, core_recv,
    bx_send, bx_recv, bz_send, bz_recv, l_send, l_recv,
    hx_send, hx_recv, hz_send, hz_recv, hy_send, hy_recv, gz_send, gz_recv, gx_send, gx_recv,
):
    s = lax.axis_index("src")
    g = lax.axis_index("gx")
    r = lax.axis_index("gy")
    core, yl = g % 2, g // 2
    z, yh = r // 2, r % 2
    me = s * d.GX + g
    X, Y, Z, N, C, CY = d.X, d.Y, d.Z, d.N, d.c, d.cy

    loads = [
        pltpu.make_async_copy(src, dst, in_sem.at[k])
        for k, (src, dst) in enumerate(
            [(act_h, act), (tsrc_h, tvec), (tsrc_h, tsrc), (wconv_h, wconv), (hup_h, hup),
             (hout_h, hout), (lidar_h, lidar), (cot_h, cot), (cam.at[me], arrived.at[me])]
        )
    ]

    order = (3, 2, 1, 0) if d.YL == 4 else range(d.YL - 1, -1, -1)

    def a_peer(far, step):
        to_s = (s + step // 2) % X
        if d.YL == 4:
            to_yl = {3: 3 - yl, 2: (yl + 2) % 4, 1: yl + 1 - 2 * (yl % 2), 0: yl}[far]
        else:
            to_yl = (yl + far) % d.YL
        to_g = to_yl * 2 + (core + step) % 2
        return to_s * d.GX + to_g, (to_s, to_g, r)

    def each_peer(body):
        for far in order:
            if far:
                body(far, 0)

        def rest(step, _):
            for far in order:
                body(far, step)
            return 0

        lax.fori_loop(1, 2 * X, rest, 0)

    def z_peer(step):
        return (s, g, ((z + step) % Z) * 2 + yh)

    def x_peer(step):
        return ((s + step) % X, g, r)

    def y_peer(step):
        at = (yl * 2 + yh + step) % Y
        return (s, (at // 2) * 2 + core, z * 2 + at % 2)

    other_core = (s, yl * 2 + 1 - core, r)

    my_block = (s * d.GX + g) * d.GY + r
    group = my_block // Y
    from_core, from_x, from_z = group // (X * Z), (group // Z) % X, group % Z
    my_y = yl * 2 + yh
    first_block = ((core * X + s) * Z + z) * Y

    def owner(block):
        return (block // (d.GX * d.GY), (block // d.GY) % d.GX, block % d.GY)

    def last_sender(at):
        return (from_x, (at // 2) * 2 + from_core, from_z * 2 + at % 2)

    self_group = jnp.logical_and(
        jnp.logical_and(from_core == core, from_z == z), from_x == s
    )

    barrier = pltpu.get_barrier_semaphore()

    def greet(device):
        pl.semaphore_signal(barrier, inc=1, device_id=device, device_id_type=MESH)

    each_peer(lambda far, step: greet(a_peer(far, step)[1]))
    count = N - 1
    for step in range(1, Z):
        greet(z_peer(step))
        count += 1
    for at in range(d.YL):
        greet((s, at * 2 + core, z * 2 + 1 - yh))
        count += 1
    for side in (-1, 1):
        for near in (-1, 0, 1):
            greet((s, (g + near + d.GX) % d.GX, (r + side + d.GY) % d.GY))
            count += 1
    for at in range(Y):
        is_self = jnp.logical_and(self_group, my_y == at)

        @pl.when(jnp.logical_not(is_self))
        def _():
            greet(last_sender(at))

    count = count + Y - jnp.where(self_group, 1, 0)
    pl.semaphore_wait(barrier, count)

    def a_start(far, step):
        to, device = a_peer(far, step)
        rcopy(cam.at[to], arrived.at[me], a_send, a_recv, device).start()

    each_peer(a_start)
    for load in loads:
        load.start()

    for load in loads[:6]:
        load.wait()
    at_y = lax.broadcasted_iota(jnp.int32, (CY, d.ty), 0) // 4
    at_q = lax.broadcasted_iota(jnp.int32, (CY, d.ty), 1)
    for p in range(d.tx):
        row = act[p : p + 1, :].astype(F32)
        column = jnp.sum(jnp.where(at_y == at_q, row, 0.0), axis=1, keepdims=True)
        mask[p] = jnp.broadcast_to(column, (CY, C))
    eye = lax.broadcasted_iota(jnp.int32, (d.ty, d.ty), 0) == lax.broadcasted_iota(
        jnp.int32, (d.ty, d.ty), 1
    )
    at_t = lax.broadcasted_iota(jnp.int32, (d.ty, 128), 0)
    at_s = lax.broadcasted_iota(jnp.int32, (d.ty, 128), 1)
    found = jnp.zeros((1, 128), jnp.int32)
    for p in range(d.tx):
        column = jnp.sum(jnp.where(eye, tvec[p : p + 1, :], 0), axis=1, keepdims=True)
        hit = jnp.where(column == at_s, at_t + p * d.ty, 0)
        found = jnp.maximum(found, jnp.max(hit, axis=0, keepdims=True))
    inv_v[...] = jnp.broadcast_to(found, (8, 128))
    inv_copy = pltpu.make_async_copy(inv_v, inv, in_sem.at[0])
    inv_copy.start()
    for i in range(3):
        for j in range(3):
            tap = wconv[2 - i, (2 - j) * C : (3 - j) * C, :].astype(F32)
            wt[i, j * C : (j + 1) * C, :] = tap.T.astype(BF16)
    hup_t[...] = hup[...].astype(F32).T.astype(BF16)
    hout_t[...] = hout[...].astype(F32).T.astype(BF16)

    inv_copy.wait()
    for load in loads[6:]:
        load.wait()
    all_but_one = pl.ds(0, N - 1)
    rcopy(
        arrived.at[all_but_one], arrived.at[all_but_one], a_send, a_recv, other_core
    ).wait_recv()

    span = 4 * CY

    def merge(p, _):
        for q in range(d.ty):
            at = tsrc[p, q]
            tile = arrived[at // 2, at % 2].astype(F32)
            for dx in range(4):
                m32[4 * p + dx, 4 * q : 4 * q + 4, :] = tile[4 * dx : 4 * dx + 4]
        for dx in range(4):
            x = 4 * p + dx
            line = pl.ds(pl.multiple_of(x * CY, CY), CY)
            m32[x] = mask[p] * (m32[x] + lidar[line, :].astype(F32))
        return 0

    lax.fori_loop(0, d.tx, merge, 0)

    def send_all(parts, slots, size, here, peer, send_sem, recv_sem):
        for k in range(1, size):
            rcopy(parts.at[(here + k) % size], slots.at[k - 1], send_sem, recv_sem, peer(k)).start()
        return rcopy(slots, slots, send_sem, recv_sem, other_core)

    def halo_start(k):
        rows_s[k, 0] = m32[0].astype(BF16)
        rows_s[k, 1] = m32[d.cx - 1].astype(BF16)
        cols_s[k, 0, 0 : d.cx, :] = m32[:, 0, :].astype(BF16)
        cols_s[k, 1, 0 : d.cx, :] = m32[:, CY - 1, :].astype(BF16)
        for side, step in ((0, -1), (1, 1)):
            for near in (-1, 0, 1):
                device = (s, (g + near + d.GX) % d.GX, (r + step + d.GY) % d.GY)
                rcopy(
                    cols_s.at[k, side], cols_r.at[k, 1 - side, 1 - near], col_send.at[k],
                    col_recv.at[k], device,
                ).start()
            device = (s, (g + step + d.GX) % d.GX, r)
            rcopy(
                rows_s.at[k, side], rows_r.at[k, 1 - side], row_send.at[k], row_recv.at[k], device
            ).start()

    at_row = lax.broadcasted_iota(jnp.int32, (CY, C), 0)
    head_row = lax.broadcasted_iota(jnp.int32, (16, C), 0)

    def put(out3, x, line, left, right):
        down = jnp.where(at_row == 0, left, pltpu.roll(line, 1, 0))
        up = jnp.where(at_row == CY - 1, right, pltpu.roll(line, CY - 1, 0))
        out3[x * CY : (x + 1) * CY, 0:C] = down.astype(BF16)
        out3[x * CY : (x + 1) * CY, C : 2 * C] = line.astype(BF16)
        out3[x * CY : (x + 1) * CY, 2 * C : 3 * C] = up.astype(BF16)

    def put_ends(out3, x, left, right):
        top = m32[x - 1, 0:16, :]
        low = m32[x - 1, CY - 16 : CY, :]
        down = jnp.where(head_row == 0, left, pltpu.roll(top, 1, 0))
        up = jnp.where(head_row == 15, right, pltpu.roll(low, 15, 0))
        out3[x * CY : x * CY + 16, 0:C] = down.astype(BF16)
        out3[(x + 1) * CY - 16 : (x + 1) * CY, 2 * C : 3 * C] = up.astype(BF16)

    def halo_inner(out3):
        for x in range(d.cx):
            put(out3, x + 1, m32[x], 0.0, 0.0)

    def halo_finish(k, out3, ends):
        rcopy(rows_s.at[k], rows_r.at[k], row_send.at[k], row_recv.at[k], other_core).wait_recv()
        rcopy(cols_r.at[k], cols_r.at[k], col_send.at[k], col_recv.at[k], other_core).wait_recv()
        ok_g = (g > 0, g < d.GX - 1)
        ok_r = (r > 0, r < d.GY - 1)
        lefts = [jnp.where(ok_r[0], cols_r[k, 0, near].astype(F32), 0.0) for near in range(3)]
        rights = [jnp.where(ok_r[1], cols_r[k, 1, near].astype(F32), 0.0) for near in range(3)]
        for side, x, row in ((0, 0, d.cx - 1), (1, d.cx + 1, 0)):
            line = rows_r[k, side].astype(F32)
            near = 0 if side == 0 else 2
            line, left, right = [
                jnp.where(ok_g[side], value, 0.0)
                for value in (line, lefts[near][row : row + 1], rights[near][row : row + 1])
            ]
            put(out3, x, line, left, right)
        for x in range(d.cx):
            left, right = lefts[1][x : x + 1], rights[1][x : x + 1]
            if ends:
                put_ends(out3, x + 1, left, right)

    def conv_inner(from3, weight):
        from3[0:CY, :] = jnp.zeros((CY, 3 * C), BF16)
        from3[(d.cx + 1) * CY :, :] = jnp.zeros((CY, 3 * C), BF16)

        def chunk(p, _):
            acc = jnp.zeros((span, C), F32)
            for i in range(3):
                start = pl.multiple_of(p * span + i * CY, CY)
                acc = acc + dot(from3[pl.ds(start, span), :], weight[i])
            conv[pl.ds(4 * p, 4)] = acc.reshape(4, CY, C)
            return 0

        lax.fori_loop(0, d.tx, chunk, 0, unroll=True)

    def conv_edges(k, from3, weight):
        conv[0] = conv[0] + dot(from3[0:CY, :], weight[0])
        conv[d.cx - 1] = conv[d.cx - 1] + dot(from3[(d.cx + 1) * CY :, :], weight[2])
        at = lax.broadcasted_iota(jnp.int32, (d.colp, C), 0)
        for side, y, ok in ((0, 0, r > 0), (1, CY - 1, r < d.GY - 1)):
            line = cols_r[k, side, 1].astype(F32)
            line = jnp.where(jnp.logical_and(ok, at < d.cx), line, 0.0).astype(BF16)
            tap = 2 * side
            before, here, after = [
                dot(line, weight[i, tap * C : (tap + 1) * C, :]) for i in range(3)
            ]
            before = jnp.where(at == 0, 0.0, pltpu.roll(before, 1, 0))
            after = jnp.where(at == d.colp - 1, 0.0, pltpu.roll(after, d.colp - 1, 0))
            total = before + here + after
            conv[:, y, :] = conv[:, y, :] + total[0 : d.cx]

    halo_start(0)
    halo_inner(m3)
    conv_inner(m3, wconv)
    halo_finish(0, m3, True)
    conv_edges(0, m3, wconv)

    def forward(p, _):
        here = pl.ds(pl.multiple_of(p * span, span), span)
        pre = conv[pl.ds(4 * p, 4)].reshape(span, C)
        occupied = jnp.concatenate([mask[p]] * 4, axis=0)
        sig = sigmoid(pre)
        feature = (occupied * (pre * sig)).astype(BF16)
        slope = occupied * (sig * (1.0 + pre * (1.0 - sig)))
        feat[here, :] = feature
        lines = pl.ds(4 * p, 4)
        m32[lines] = slope.reshape(4, CY, C)
        up = dot(feature, hup[...])
        sig = sigmoid(up)
        hidden = (up * sig).astype(BF16)
        hid[here, :] = hidden
        maps[here, :] = dot(hidden, hout[...]).astype(BF16)
        grad = (dot(cot[here, :], hout_t[...]) * (sig * (1.0 + up * (1.0 - sig)))).astype(BF16)
        gh[here, :] = grad
        value = dot(grad, hup_t[...]) * m32[lines].reshape(span, C)
        m32[lines] = value.reshape(4, CY, C)
        gp[here, :] = value.astype(BF16)
        return 0

    lax.fori_loop(0, d.tx, forward, 0, unroll=True)
    halo_start(1)
    maps_out = pltpu.make_async_copy(maps, maps_o, out_sem.at[0])
    maps_out.start()

    def last(total, rows):
        rows[pl.ds(0, d.rlp, stride=2), :] = total[:, 0:128]
        rows[pl.ds(1, d.rlp, stride=2), :] = total[:, 128:256]
        for k in range(Y):
            at = k
            ls[at] = rows[k * d.hb : k * d.hb + d.hbp, :].astype(BF16)
            block = first_block + k
            copy = rcopy(ls.at[at], l_r.at[my_y], l_send, l_recv, owner(block))
            local = pltpu.make_async_copy(ls.at[at], l_r.at[my_y], l_recv)

            @pl.when(block != my_block)
            def _():
                copy.start()

            @pl.when(block == my_block)
            def _():
                local.start()

    term = dot_tn(feat[...], gh[...])
    for half in range(d.head // C):
        h32[half * C : (half + 1) * C, :] = term[:, half * C : (half + 1) * C]
    base = d.head
    term = dot_tn(hid[...], cot[...])
    depth = d.head // 2
    for half in range(2):
        h32[base : base + depth, half * d.outc : (half + 1) * d.outc] = term[
            half * depth : (half + 1) * depth, :
        ]
    hb[...] = h32[...].astype(BF16)
    hmine = pl.ds(pl.multiple_of(core * d.hc, d.hc), d.hc)
    htheirs = pl.ds(pl.multiple_of((1 - core) * d.hc, d.hc), d.hc)
    hcore_copy = rcopy(hb.at[htheirs], hcore_r, core_send.at[1], core_recv.at[1], other_core)
    hcore_copy.start()

    def tap_grads(i, _):
        for j in range(3):
            term = dot_tn(
                m3[pl.ds(pl.multiple_of(i * CY, CY), d.cells), j * C : (j + 1) * C], gp[...]
            )
            at = pl.ds(pl.multiple_of(i * (3 * C) + j * C, C), C)
            dw32[at, :] = term
            dwb[at, :] = term.astype(BF16)
        return 0

    lax.fori_loop(0, 3, tap_grads, 0)
    mine = pl.ds(pl.multiple_of(core * d.rc, d.rc), d.rc)
    theirs = pl.ds(pl.multiple_of((1 - core) * d.rc, d.rc), d.rc)
    core_copy = rcopy(dwb.at[theirs], core_r, core_send.at[0], core_recv.at[0], other_core)
    core_copy.start()

    hcore_copy.wait_recv()
    hs32[...] = h32[hmine, :] + hcore_r[...].astype(F32)
    for k in range(X):
        hxs[k] = hs32[k * d.hx : (k + 1) * d.hx, :].astype(BF16)
    hx_wait = send_all(hxs, hx_r, X, s, x_peer, hx_send, hx_recv)

    halo_inner(g3)
    conv_inner(g3, wt)

    hx_wait.wait_recv()
    total = hs32[pl.ds(pl.multiple_of(s * d.hx, d.hx), d.hx), :]
    for k in range(X - 1):
        total = total + hx_r[k].astype(F32)
    hxsum[0 : d.hx, :] = total
    for k in range(Z):
        part = hxsum[k * d.hz : k * d.hz + d.hzp, :]
        hzs32[k] = part
        hzs[k] = part.astype(BF16)
    hz_wait = send_all(hzs, hz_r, Z, z, z_peer, hz_send, hz_recv)

    core_copy.wait_recv()
    cs32[...] = dw32[mine, :] + core_r[...].astype(F32)
    for k in range(X):
        bx[k] = cs32[k * d.bx : (k + 1) * d.bx, :].astype(BF16)
    bx_wait = send_all(bx, bx_r, X, s, x_peer, bx_send, bx_recv)

    halo_finish(1, g3, False)
    conv_edges(1, g3, wt)

    def backward(p, _):
        here = pl.ds(pl.multiple_of(p * span, span), span)
        acc = conv[pl.ds(4 * p, 4)].reshape(span, C)
        acc = acc * jnp.concatenate([mask[p]] * 4, axis=0)
        gi[here, :] = acc.astype(BF16)
        m32[pl.ds(4 * p, 4)] = acc.reshape(4, CY, C)
        for q in range(d.ty):
            parts = [m32[4 * p + dx, 4 * q : 4 * q + 4, :] for dx in range(4)]
            tiles[p * d.ty + q] = jnp.concatenate(parts, axis=0).astype(BF16)
        return 0

    lax.fori_loop(0, d.tx, backward, 0, unroll=True)
    gin_out = pltpu.make_async_copy(gi, gin_o, out_sem.at[1])
    gin_out.start()

    hz_wait.wait_recv()
    total = hzs32[z]
    for k in range(Z - 1):
        total = total + hz_r[k].astype(F32)
    hy[...] = total.astype(BF16)
    for k in range(1, Y):
        rcopy(hy, hy_r.at[k - 1], hy_send, hy_recv, y_peer(k)).start()
    hy_wait = rcopy(hy_r, hy_r, hy_send, hy_recv, other_core)

    def b_start(far, step):
        to, device = a_peer(far, step)
        for slot in range(2):
            ret[to, slot] = tiles[inv[0, to * 2 + slot]]
        rcopy(ret.at[to], gcam_o.at[me], b_send, b_recv, device).start()

    each_peer(b_start)
    for slot in range(2):
        ret[me, slot] = tiles[inv[0, me * 2 + slot]]
    own_out = pltpu.make_async_copy(ret.at[me], gcam_o.at[me], out_sem.at[2])
    own_out.start()

    hy_wait.wait_recv()
    total = hy[...].astype(F32)
    for k in range(Y - 1):
        total = total + hy_r[k].astype(F32)
    hpart[z] = total.astype(BF16)
    part = hpart.at[z]
    for k in range(1, Z):
        rcopy(part, part, gz_send, gz_recv, z_peer(k)).start()

    bx_wait.wait_recv()
    total = cs32[pl.ds(pl.multiple_of(s * d.bx, 8), d.bx), :]
    for k in range(X - 1):
        total = total + bx_r[k].astype(F32)
    bxsum[0 : d.bx, :] = total
    for k in range(Z):
        part = bxsum[k * d.rl : k * d.rl + d.rlp, :]
        bz32[k] = part
        bz[k] = part.astype(BF16)
    bz_wait = send_all(bz, bz_r, Z, z, z_peer, bz_send, bz_recv)

    parts = hpart.at[pl.ds(0, Z - 1)]
    gz_wait = rcopy(parts, parts, gz_send, gz_recv, other_core)
    gz_wait.wait_recv()
    for k in range(Z):
        hpack[k * d.hz : k * d.hz + d.hzp, :] = hpart[k].astype(F32)
    hall[core, s] = hpack[0 : d.hx, :].astype(BF16)
    part = hall.at[core, s]
    for k in range(1, X):
        rcopy(part, part, gx_send, gx_recv, x_peer(k)).start()

    bz_wait.wait_recv()
    total = bz32[z]
    for k in range(Z - 1):
        total = total + bz_r[k].astype(F32)
    last(total, brow)
    parts = hall.at[core, pl.ds(0, X - 1)]
    gx_wait = rcopy(parts, parts, gx_send, gx_recv, other_core)
    gx_wait.wait_recv()
    gcore = rcopy(hall.at[core], hall.at[core], core_send.at[2], core_recv.at[2], other_core)
    gcore.start()

    total = jnp.zeros((d.hbp, 128), F32)
    pltpu.make_async_copy(ls, l_r, l_recv).wait()
    for k in range(Y):
        total = total + l_r[k].astype(F32)
    gconv_o[...] = total[0 : d.hb, :] * d.scale

    rcopy(
        hall.at[1 - core], hall.at[1 - core], core_send.at[2], core_recv.at[2], other_core
    ).wait_recv()
    for c in range(2):
        for x in range(X):
            at = c * d.hc + x * d.hx
            h32[at : at + d.hx, :] = hall[c, x].astype(F32)
    for half in range(d.head // C):
        gup_o[:, half * C : (half + 1) * C] = h32[half * C : (half + 1) * C, :] * d.scale
    for half in range(2):
        gout_o[half * depth : (half + 1) * depth, :] = (
            h32[base : base + depth, half * d.outc : (half + 1) * d.outc] * d.scale
        )

    parts = ret.at[all_but_one]
    b_wait = rcopy(parts, gcam_o.at[all_but_one], b_send, b_recv, other_core)
    b_wait.wait_recv()

    rcopy(parts, parts, a_send, a_recv, other_core).wait_send()
    b_wait.wait_send()
    for k in range(2):
        rcopy(rows_s.at[k], rows_r.at[k], row_send.at[k], row_recv.at[k], other_core).wait_send()
        rcopy(cols_r.at[k], cols_r.at[k], col_send.at[k], col_recv.at[k], other_core).wait_send()
    for wait in (
        bx_wait, bz_wait, hx_wait, hz_wait, hy_wait, gz_wait, gx_wait,
        core_copy, hcore_copy, gcore,
    ):
        wait.wait_send()

    @pl.when(self_group)
    def _():
        parts = ls.at[pl.ds(0, Y - 1)]
        rcopy(parts, parts, l_send, l_recv, other_core).wait_send()

    @pl.when(jnp.logical_not(self_group))
    def _():
        rcopy(ls, ls, l_send, l_recv, other_core).wait_send()

    maps_out.wait()
    gin_out.wait()
    own_out.wait()


def copy_kernel(*refs):
    loads = [
        pltpu.make_async_copy(refs[k], refs[12 + k], refs[18].at[k]) for k in range(6)
    ]
    stores = [
        pltpu.make_async_copy(refs[12 + k], refs[6 + k], refs[18].at[k]) for k in range(6)
    ]
    for load in loads:
        load.start()
    for load, store in zip(loads, stores):
        load.wait()
        store.start()
    for store in stores:
        store.wait()


def per_device(
    cam_send, lidar_bev, tile_active, tile_source, conv_weight, head_up, head_out, cotangent
):
    channels = cam_send.shape[5]
    cells_x, cells_y = lidar_bev.shape[1], lidar_bev.shape[2]
    head, outc = head_out.shape
    d = Dims(
        lax.axis_size("src"), lax.axis_size("gx"), lax.axis_size("gy"),
        cells_x, cells_y, channels, head, outc,
    )
    C, X, Y, Z, N = d.c, d.X, d.Y, d.Z, d.N
    cells = d.cells
    vmem = pl.BlockSpec(memory_space=pltpu.VMEM)
    anyw = pl.BlockSpec(memory_space=pl.ANY)
    dma = pltpu.SemaphoreType.DMA

    def b16(*shape):
        return pltpu.VMEM(shape, BF16)

    def f32(*shape):
        return pltpu.VMEM(shape, F32)

    def i32(*shape):
        return pltpu.VMEM(shape, jnp.int32)

    scratch = [
        b16(N, 2, 16, C), b16(cells, C), b16(3, 3 * C, C), b16(C, head), b16(head, outc),
        b16(cells, outc), i32(d.tx, d.ty), i32(d.tx, d.ty), pltpu.SMEM((d.tx, d.ty), jnp.int32),
        i32(8, 128), pltpu.SMEM((8, 128), jnp.int32),
        b16(3, 3 * C, C), b16(head, C), b16(outc, head), f32(d.tx, cells_y, C),
        f32(cells_x, cells_y, C), f32(cells_x, cells_y, C),
        b16((cells_x + 2) * cells_y, 3 * C), b16((cells_x + 2) * cells_y, 3 * C),
        b16(2, 2, cells_y, C), b16(2, 2, cells_y, C),
        b16(2, 2, d.colp, C), b16(2, 2, 3, d.colp, C),
        b16(cells, C), b16(cells, head), b16(cells, head), b16(cells, outc), b16(cells, C),
        b16(cells, C), b16(d.tiles, 16, C), b16(N, 2, 16, C),
        f32(d.rows, C), b16(d.rows, C), b16(d.rc, C), f32(d.rc, C),
        b16(X, d.bx, C), b16(X - 1, d.bx, C), f32(d.bx + d.rlp, C),
        f32(Z, d.rlp, C), b16(Z, d.rlp, C), b16(Z - 1, d.rlp, C), f32(2 * d.rlp + 16, 128),
        b16(Y, d.hbp, 128), b16(Y, d.hbp, 128),
        f32(d.hrows, C), b16(d.hrows, C), b16(d.hc, C), f32(d.hc, C),
        b16(X, d.hx, C), b16(X - 1, d.hx, C), f32(d.hx + 16, C),
        f32(Z, d.hzp, C), b16(Z, d.hzp, C), b16(Z - 1, d.hzp, C),
        b16(d.hzp, C), b16(Y - 1, d.hzp, C),
        b16(Z, d.hzp, C), f32(d.hx + 16, C), b16(2, X, d.hx, C),
        dma((9,)), dma((3,)),
        dma, dma, dma, dma, dma((2,)), dma((2,)), dma((2,)), dma((2,)), dma((3,)), dma((3,)),
        *[dma] * 16,
    ]
    results = pl.pallas_call(
        functools.partial(kernel, d),
        out_shape=(
            jax.ShapeDtypeStruct((cells, outc), BF16),
            jax.ShapeDtypeStruct((cells, C), BF16),
            jax.ShapeDtypeStruct((N, 2, 16, C), BF16),
            jax.ShapeDtypeStruct((d.hb, 128), F32),
            jax.ShapeDtypeStruct((C, head), F32),
            jax.ShapeDtypeStruct((head, outc), F32),
        ),
        in_specs=[anyw] * 8,
        out_specs=(anyw, anyw, anyw, vmem, vmem, vmem),
        scratch_shapes=scratch,
        compiler_params=pltpu.CompilerParams(
            collective_id=0, has_side_effects=True, vmem_limit_bytes=64 * 1024 * 1024
        ),
    )(
        cam_send.reshape(N, 2, 16, C),
        lidar_bev.reshape(cells, C),
        tile_active.reshape(d.tx, d.ty),
        tile_source.reshape(d.tx, d.ty),
        conv_weight.reshape(3, 3 * C, C),
        head_up,
        head_out,
        cotangent.reshape(cells, outc),
    )
    maps, gin, gcam, gconv, gup, gout = pl.pallas_call(
        copy_kernel,
        out_shape=tuple(jax.ShapeDtypeStruct(a.shape, a.dtype) for a in results),
        in_specs=[anyw] * 6,
        out_specs=(anyw,) * 6,
        scratch_shapes=[*[pltpu.VMEM(a.shape, a.dtype) for a in results], dma((6,))],
        compiler_params=pltpu.CompilerParams(vmem_limit_bytes=64 * 1024 * 1024),
    )(*results)
    return (
        maps.reshape(1, cells_x, cells_y, outc),
        gin.reshape(1, cells_x, cells_y, C),
        gcam.reshape(1, 1, N, 2, 16, C),
        gconv.reshape(-1),
        gup,
        gout,
    )


def solution(mesh):
    in_specs = (
        P(("src", "gx"), "gy", None, None, None, None),
        P("src", "gx", "gy", None),
        P("src", "gx", "gy"),
        P("src", "gx", "gy"),
        P(),
        P(),
        P(),
        P("src", "gx", "gy", None),
    )
    out_specs = (
        P("src", "gx", "gy", None),
        P("src", "gx", "gy", None),
        P(("src", "gx"), "gy", None, None, None, None),
        P(("src", "gx", "gy")),
        P(),
        P(),
    )
    return jax.shard_map(
        per_device, mesh=mesh, in_specs=in_specs, out_specs=out_specs, check_vma=False
    )
```

```python
import functools
import math

import jax
import jax.numpy as jnp
from jax import lax
from jax.experimental import pallas as pl
from jax.experimental.pallas import tpu as pltpu
from jax.sharding import PartitionSpec as P

MESH = pl.DeviceIdType.MESH
F32 = jnp.float32
BF16 = jnp.bfloat16
VMEM_BYTES = (62 * 1024 - 256) * 1024


def pad16(rows):
    return (rows + 15) // 16 * 16


def sigmoid(value):
    return 0.5 * jnp.tanh(0.5 * value) + 0.5


def dot(lhs, rhs):
    return jnp.dot(lhs, rhs, preferred_element_type=F32)


def dot_tn(lhs, rhs):
    return lax.dot_general(lhs, rhs, (((0,), (0,)), ((), ())), preferred_element_type=F32)


def rcopy(src, dst, send_sem, recv_sem, device):
    return pltpu.make_async_remote_copy(
        src_ref=src,
        dst_ref=dst,
        send_sem=send_sem,
        recv_sem=recv_sem,
        device_id=device,
        device_id_type=MESH,
    )


class Dims:
    def __init__(self, n_src, n_gx, n_gy, cells_x, cells_y, channels, head, outc):
        self.X, self.GX, self.GY = n_src, n_gx, n_gy
        self.YL, self.Z, self.Y = n_gx // 2, n_gy // 2, n_gx
        self.N = n_src * n_gx
        self.cx, self.cy, self.c = cells_x, cells_y, channels
        self.cells = cells_x * cells_y
        self.tx, self.ty = cells_x // 4, cells_y // 4
        self.tiles = self.tx * self.ty
        self.head, self.outc = head, outc
        self.colp = pad16(cells_x)
        self.rows = 9 * channels
        self.rc = self.rows // 2
        self.bx = self.rc // self.X
        self.rl = self.bx // self.Z
        self.rlp = pad16(self.rl)
        self.hb = 2 * self.rl // self.Y
        self.hbp = pad16(self.hb)
        self.hrows = (channels * head + head * outc) // channels
        self.hc = self.hrows // 2
        self.hx = self.hc // self.X
        self.hz = self.hx // self.Z
        self.hzp = pad16(self.hz)
        self.scale = 1.0 / math.sqrt(n_src * n_gx * n_gy * cells_x * cells_y)


def kernel(
    d,
    cam, lidar_h, act_h, tsrc_h, wconv_h, hup_h, hout_h, cot_h,
    maps_o, gin_o, gcam_o, gconv_o, gup_o, gout_o,
    arrived, lidar, wconv, hup, hout, cot, act, tvec, tsrc, inv_v, inv,
    wt, hup_t, hout_t, mask,
    m32, conv, m3, g3, rows_s, rows_r, cols_s, cols_r,
    feat, hid, gh, gp, tiles, ret,
    dw32, dwb, core_r, cs32,
    bx, bx_r, bxsum, bz32, bz, bz_r, brow, ls, l_r,
    h32, hb, hcore_r, hs32, hxs, hx_r, hxsum, hzs32, hzs, hz_r, hy, hy_r, hpart, hpack, hall,
    in_sem, out_sem,
    a_send, a_recv, b_send, b_recv, row_send, row_recv, col_send, col_recv, core_send, core_recv,
    bx_send, bx_recv, bz_send, bz_recv, l_send, l_recv,
    hx_send, hx_recv, hz_send, hz_recv, hy_send, hy_recv, gz_send, gz_recv, gx_send, gx_recv,
):
    s = lax.axis_index("src")
    g = lax.axis_index("gx")
    r = lax.axis_index("gy")
    core, yl = g % 2, g // 2
    z, yh = r // 2, r % 2
    me = s * d.GX + g
    X, Y, Z, N, C, CY = d.X, d.Y, d.Z, d.N, d.c, d.cy

    loads = [
        pltpu.make_async_copy(src, dst, in_sem.at[k])
        for k, (src, dst) in enumerate(
            [(act_h, act), (tsrc_h, tvec), (tsrc_h, tsrc), (wconv_h, wconv), (hup_h, hup),
             (hout_h, hout), (lidar_h, lidar), (cot_h, cot), (cam.at[me], arrived.at[me])]
        )
    ]

    order = (3, 2, 1, 0) if d.YL == 4 else range(d.YL - 1, -1, -1)

    def a_peer(far, step):
        to_s = (s + step // 2) % X
        if d.YL == 4:
            to_yl = {3: 3 - yl, 2: (yl + 2) % 4, 1: yl + 1 - 2 * (yl % 2), 0: yl}[far]
        else:
            to_yl = (yl + far) % d.YL
        to_g = to_yl * 2 + (core + step) % 2
        return to_s * d.GX + to_g, (to_s, to_g, r)

    def each_peer(body):
        for far in order:
            if far:
                body(far, 0)

        def rest(step, _):
            for far in order:
                body(far, step)
            return 0

        lax.fori_loop(1, 2 * X, rest, 0)

    def z_peer(step):
        return (s, g, ((z + step) % Z) * 2 + yh)

    def x_peer(step):
        return ((s + step) % X, g, r)

    def y_peer(step):
        at = (yl * 2 + yh + step) % Y
        return (s, (at // 2) * 2 + core, z * 2 + at % 2)

    other_core = (s, yl * 2 + 1 - core, r)

    my_block = (s * d.GX + g) * d.GY + r
    group = my_block // Y
    from_core, from_x, from_z = group // (X * Z), (group // Z) % X, group % Z
    my_y = yl * 2 + yh
    first_block = ((core * X + s) * Z + z) * Y

    def owner(block):
        return (block // (d.GX * d.GY), (block // d.GY) % d.GX, block % d.GY)

    def last_sender(at):
        return (from_x, (at // 2) * 2 + from_core, from_z * 2 + at % 2)

    self_group = jnp.logical_and(
        jnp.logical_and(from_core == core, from_z == z), from_x == s
    )

    barrier = pltpu.get_barrier_semaphore()

    def greet(device):
        pl.semaphore_signal(barrier, inc=1, device_id=device, device_id_type=MESH)

    each_peer(lambda far, step: greet(a_peer(far, step)[1]))
    count = N - 1
    for step in range(1, Z):
        greet(z_peer(step))
        count += 1
    for at in range(d.YL):
        greet((s, at * 2 + core, z * 2 + 1 - yh))
        count += 1
    for side in (-1, 1):
        for near in (-1, 0, 1):
            greet((s, (g + near + d.GX) % d.GX, (r + side + d.GY) % d.GY))
            count += 1
    for at in range(Y):
        is_self = jnp.logical_and(self_group, my_y == at)

        @pl.when(jnp.logical_not(is_self))
        def _():
            greet(last_sender(at))

    count = count + Y - jnp.where(self_group, 1, 0)
    pl.semaphore_wait(barrier, count)

    def a_start(far, step):
        to, device = a_peer(far, step)
        rcopy(cam.at[to], arrived.at[me], a_send, a_recv, device).start()

    each_peer(a_start)
    for load in loads:
        load.start()

    for load in loads[:6]:
        load.wait()
    at_y = lax.broadcasted_iota(jnp.int32, (CY, d.ty), 0) // 4
    at_q = lax.broadcasted_iota(jnp.int32, (CY, d.ty), 1)
    for p in range(d.tx):
        row = act[p : p + 1, :].astype(F32)
        column = jnp.sum(jnp.where(at_y == at_q, row, 0.0), axis=1, keepdims=True)
        mask[p] = jnp.broadcast_to(column, (CY, C))
    eye = lax.broadcasted_iota(jnp.int32, (d.ty, d.ty), 0) == lax.broadcasted_iota(
        jnp.int32, (d.ty, d.ty), 1
    )
    at_t = lax.broadcasted_iota(jnp.int32, (d.ty, 128), 0)
    at_s = lax.broadcasted_iota(jnp.int32, (d.ty, 128), 1)
    found = jnp.zeros((1, 128), jnp.int32)
    for p in range(d.tx):
        column = jnp.sum(jnp.where(eye, tvec[p : p + 1, :], 0), axis=1, keepdims=True)
        hit = jnp.where(column == at_s, at_t + p * d.ty, 0)
        found = jnp.maximum(found, jnp.max(hit, axis=0, keepdims=True))
    inv_v[...] = jnp.broadcast_to(found, (8, 128))
    inv_copy = pltpu.make_async_copy(inv_v, inv, in_sem.at[0])
    inv_copy.start()
    for i in range(3):
        for j in range(3):
            tap = wconv[2 - i, (2 - j) * C : (3 - j) * C, :].astype(F32)
            wt[i, j * C : (j + 1) * C, :] = tap.T.astype(BF16)
    hup_t[...] = hup[...].astype(F32).T.astype(BF16)
    hout_t[...] = hout[...].astype(F32).T.astype(BF16)

    inv_copy.wait()
    for load in loads[6:]:
        load.wait()
    all_but_one = pl.ds(0, N - 1)
    rcopy(
        arrived.at[all_but_one], arrived.at[all_but_one], a_send, a_recv, other_core
    ).wait_recv()

    span = 4 * CY

    def merge(p, _):
        for q in range(d.ty):
            at = tsrc[p, q]
            tile = arrived[at // 2, at % 2].astype(F32)
            for dx in range(4):
                m32[4 * p + dx, 4 * q : 4 * q + 4, :] = tile[4 * dx : 4 * dx + 4]
        for dx in range(4):
            x = 4 * p + dx
            line = pl.ds(pl.multiple_of(x * CY, CY), CY)
            m32[x] = mask[p] * (m32[x] + lidar[line, :].astype(F32))
        return 0

    lax.fori_loop(0, d.tx, merge, 0)

    def send_all(parts, slots, size, here, peer, send_sem, recv_sem):
        for k in range(1, size):
            rcopy(parts.at[(here + k) % size], slots.at[k - 1], send_sem, recv_sem, peer(k)).start()
        return rcopy(slots, slots, send_sem, recv_sem, other_core)

    def halo_start(k):
        rows_s[k, 0] = m32[0].astype(BF16)
        rows_s[k, 1] = m32[d.cx - 1].astype(BF16)
        cols_s[k, 0, 0 : d.cx, :] = m32[:, 0, :].astype(BF16)
        cols_s[k, 1, 0 : d.cx, :] = m32[:, CY - 1, :].astype(BF16)
        for side, step in ((0, -1), (1, 1)):
            for near in (-1, 0, 1):
                device = (s, (g + near + d.GX) % d.GX, (r + step + d.GY) % d.GY)
                rcopy(
                    cols_s.at[k, side], cols_r.at[k, 1 - side, 1 - near], col_send.at[k],
                    col_recv.at[k], device,
                ).start()
            device = (s, (g + step + d.GX) % d.GX, r)
            rcopy(
                rows_s.at[k, side], rows_r.at[k, 1 - side], row_send.at[k], row_recv.at[k], device
            ).start()

    at_row = lax.broadcasted_iota(jnp.int32, (CY, C), 0)
    head_row = lax.broadcasted_iota(jnp.int32, (16, C), 0)

    def put(out3, x, line, left, right):
        down = jnp.where(at_row == 0, left, pltpu.roll(line, 1, 0))
        up = jnp.where(at_row == CY - 1, right, pltpu.roll(line, CY - 1, 0))
        out3[x * CY : (x + 1) * CY, 0:C] = down.astype(BF16)
        out3[x * CY : (x + 1) * CY, C : 2 * C] = line.astype(BF16)
        out3[x * CY : (x + 1) * CY, 2 * C : 3 * C] = up.astype(BF16)

    def put_ends(out3, x, left, right):
        top = m32[x - 1, 0:16, :]
        low = m32[x - 1, CY - 16 : CY, :]
        down = jnp.where(head_row == 0, left, pltpu.roll(top, 1, 0))
        up = jnp.where(head_row == 15, right, pltpu.roll(low, 15, 0))
        out3[x * CY : x * CY + 16, 0:C] = down.astype(BF16)
        out3[(x + 1) * CY - 16 : (x + 1) * CY, 2 * C : 3 * C] = up.astype(BF16)

    def halo_inner(out3):
        for x in range(d.cx):
            put(out3, x + 1, m32[x], 0.0, 0.0)

    def halo_finish(k, out3, ends):
        rcopy(rows_s.at[k], rows_r.at[k], row_send.at[k], row_recv.at[k], other_core).wait_recv()
        rcopy(cols_r.at[k], cols_r.at[k], col_send.at[k], col_recv.at[k], other_core).wait_recv()
        ok_g = (g > 0, g < d.GX - 1)
        ok_r = (r > 0, r < d.GY - 1)
        lefts = [jnp.where(ok_r[0], cols_r[k, 0, near].astype(F32), 0.0) for near in range(3)]
        rights = [jnp.where(ok_r[1], cols_r[k, 1, near].astype(F32), 0.0) for near in range(3)]
        for side, x, row in ((0, 0, d.cx - 1), (1, d.cx + 1, 0)):
            line = rows_r[k, side].astype(F32)
            near = 0 if side == 0 else 2
            line, left, right = [
                jnp.where(ok_g[side], value, 0.0)
                for value in (line, lefts[near][row : row + 1], rights[near][row : row + 1])
            ]
            put(out3, x, line, left, right)
        for x in range(d.cx):
            left, right = lefts[1][x : x + 1], rights[1][x : x + 1]
            if ends:
                put_ends(out3, x + 1, left, right)

    def conv_inner(from3, weight):
        from3[0:CY, :] = jnp.zeros((CY, 3 * C), BF16)
        from3[(d.cx + 1) * CY :, :] = jnp.zeros((CY, 3 * C), BF16)

        def chunk(p, _):
            acc = jnp.zeros((span, C), F32)
            for i in range(3):
                start = pl.multiple_of(p * span + i * CY, CY)
                acc = acc + dot(from3[pl.ds(start, span), :], weight[i])
            conv[pl.ds(4 * p, 4)] = acc.reshape(4, CY, C)
            return 0

        lax.fori_loop(0, d.tx, chunk, 0, unroll=True)

    def conv_edges(k, from3, weight):
        conv[0] = conv[0] + dot(from3[0:CY, :], weight[0])
        conv[d.cx - 1] = conv[d.cx - 1] + dot(from3[(d.cx + 1) * CY :, :], weight[2])
        at = lax.broadcasted_iota(jnp.int32, (d.colp, C), 0)
        for side, y, ok in ((0, 0, r > 0), (1, CY - 1, r < d.GY - 1)):
            line = cols_r[k, side, 1].astype(F32)
            line = jnp.where(jnp.logical_and(ok, at < d.cx), line, 0.0).astype(BF16)
            tap = 2 * side
            before, here, after = [
                dot(line, weight[i, tap * C : (tap + 1) * C, :]) for i in range(3)
            ]
            before = jnp.where(at == 0, 0.0, pltpu.roll(before, 1, 0))
            after = jnp.where(at == d.colp - 1, 0.0, pltpu.roll(after, d.colp - 1, 0))
            total = before + here + after
            conv[:, y, :] = conv[:, y, :] + total[0 : d.cx]

    halo_start(0)
    halo_inner(m3)
    conv_inner(m3, wconv)
    halo_finish(0, m3, True)
    conv_edges(0, m3, wconv)

    def forward(p, _):
        here = pl.ds(pl.multiple_of(p * span, span), span)
        pre = conv[pl.ds(4 * p, 4)].reshape(span, C)
        occupied = jnp.concatenate([mask[p]] * 4, axis=0)
        sig = sigmoid(pre)
        feature = (occupied * (pre * sig)).astype(BF16)
        slope = occupied * (sig * (1.0 + pre * (1.0 - sig)))
        feat[here, :] = feature
        lines = pl.ds(4 * p, 4)
        m32[lines] = slope.reshape(4, CY, C)
        up = dot(feature, hup[...])
        sig = sigmoid(up)
        hidden = (up * sig).astype(BF16)
        hid[here, :] = hidden
        maps_o[here, :] = dot(hidden, hout[...]).astype(BF16)
        grad = (dot(cot[here, :], hout_t[...]) * (sig * (1.0 + up * (1.0 - sig)))).astype(BF16)
        gh[here, :] = grad
        value = dot(grad, hup_t[...]) * m32[lines].reshape(span, C)
        m32[lines] = value.reshape(4, CY, C)
        gp[here, :] = value.astype(BF16)
        return 0

    lax.fori_loop(0, d.tx, forward, 0, unroll=True)
    halo_start(1)
    def last(total, rows):
        rows[pl.ds(0, d.rlp, stride=2), :] = total[:, 0:128]
        rows[pl.ds(1, d.rlp, stride=2), :] = total[:, 128:256]
        for k in range(Y):
            at = k
            ls[at] = rows[k * d.hb : k * d.hb + d.hbp, :].astype(BF16)
            block = first_block + k
            copy = rcopy(ls.at[at], l_r.at[my_y], l_send, l_recv, owner(block))
            local = pltpu.make_async_copy(ls.at[at], l_r.at[my_y], l_recv)

            @pl.when(block != my_block)
            def _():
                copy.start()

            @pl.when(block == my_block)
            def _():
                local.start()

    term = dot_tn(feat[...], gh[...])
    for half in range(d.head // C):
        h32[half * C : (half + 1) * C, :] = term[:, half * C : (half + 1) * C]
    base = d.head
    term = dot_tn(hid[...], cot[...])
    depth = d.head // 2
    for half in range(2):
        h32[base : base + depth, half * d.outc : (half + 1) * d.outc] = term[
            half * depth : (half + 1) * depth, :
        ]
    hb[...] = h32[...].astype(BF16)
    hmine = pl.ds(pl.multiple_of(core * d.hc, d.hc), d.hc)
    htheirs = pl.ds(pl.multiple_of((1 - core) * d.hc, d.hc), d.hc)
    hcore_copy = rcopy(hb.at[htheirs], hcore_r, core_send.at[1], core_recv.at[1], other_core)
    hcore_copy.start()

    def tap_grads(i, _):
        for j in range(3):
            term = dot_tn(
                m3[pl.ds(pl.multiple_of(i * CY, CY), d.cells), j * C : (j + 1) * C], gp[...]
            )
            at = pl.ds(pl.multiple_of(i * (3 * C) + j * C, C), C)
            dw32[at, :] = term
            dwb[at, :] = term.astype(BF16)
        return 0

    lax.fori_loop(0, 3, tap_grads, 0)
    mine = pl.ds(pl.multiple_of(core * d.rc, d.rc), d.rc)
    theirs = pl.ds(pl.multiple_of((1 - core) * d.rc, d.rc), d.rc)
    core_copy = rcopy(dwb.at[theirs], core_r, core_send.at[0], core_recv.at[0], other_core)
    core_copy.start()

    hcore_copy.wait_recv()
    hs32[...] = h32[hmine, :] + hcore_r[...].astype(F32)
    for k in range(X):
        hxs[k] = hs32[k * d.hx : (k + 1) * d.hx, :].astype(BF16)
    hx_wait = send_all(hxs, hx_r, X, s, x_peer, hx_send, hx_recv)

    halo_inner(g3)
    conv_inner(g3, wt)

    hx_wait.wait_recv()
    total = hs32[pl.ds(pl.multiple_of(s * d.hx, d.hx), d.hx), :]
    for k in range(X - 1):
        total = total + hx_r[k].astype(F32)
    hxsum[0 : d.hx, :] = total
    for k in range(Z):
        part = hxsum[k * d.hz : k * d.hz + d.hzp, :]
        hzs32[k] = part
        hzs[k] = part.astype(BF16)
    hz_wait = send_all(hzs, hz_r, Z, z, z_peer, hz_send, hz_recv)

    core_copy.wait_recv()
    cs32[...] = dw32[mine, :] + core_r[...].astype(F32)
    for k in range(X):
        bx[k] = cs32[k * d.bx : (k + 1) * d.bx, :].astype(BF16)
    bx_wait = send_all(bx, bx_r, X, s, x_peer, bx_send, bx_recv)

    halo_finish(1, g3, False)
    conv_edges(1, g3, wt)

    def backward(p, _):
        here = pl.ds(pl.multiple_of(p * span, span), span)
        acc = conv[pl.ds(4 * p, 4)].reshape(span, C)
        acc = acc * jnp.concatenate([mask[p]] * 4, axis=0)
        gin_o[here, :] = acc.astype(BF16)
        m32[pl.ds(4 * p, 4)] = acc.reshape(4, CY, C)
        for q in range(d.ty):
            parts = [m32[4 * p + dx, 4 * q : 4 * q + 4, :] for dx in range(4)]
            tiles[p * d.ty + q] = jnp.concatenate(parts, axis=0).astype(BF16)
        return 0

    lax.fori_loop(0, d.tx, backward, 0, unroll=True)
    hz_wait.wait_recv()
    total = hzs32[z]
    for k in range(Z - 1):
        total = total + hz_r[k].astype(F32)
    hy[...] = total.astype(BF16)
    for k in range(1, Y):
        rcopy(hy, hy_r.at[k - 1], hy_send, hy_recv, y_peer(k)).start()
    hy_wait = rcopy(hy_r, hy_r, hy_send, hy_recv, other_core)

    def b_start(far, step):
        to, device = a_peer(far, step)
        for slot in range(2):
            ret[to, slot] = tiles[inv[0, to * 2 + slot]]
        rcopy(ret.at[to], gcam_o.at[me], b_send, b_recv, device).start()

    each_peer(b_start)
    for slot in range(2):
        ret[me, slot] = tiles[inv[0, me * 2 + slot]]
    own_out = pltpu.make_async_copy(ret.at[me], gcam_o.at[me], out_sem)
    own_out.start()

    hy_wait.wait_recv()
    total = hy[...].astype(F32)
    for k in range(Y - 1):
        total = total + hy_r[k].astype(F32)
    hpart[z] = total.astype(BF16)
    part = hpart.at[z]
    for k in range(1, Z):
        rcopy(part, part, gz_send, gz_recv, z_peer(k)).start()

    bx_wait.wait_recv()
    total = cs32[pl.ds(pl.multiple_of(s * d.bx, 8), d.bx), :]
    for k in range(X - 1):
        total = total + bx_r[k].astype(F32)
    bxsum[0 : d.bx, :] = total
    for k in range(Z):
        part = bxsum[k * d.rl : k * d.rl + d.rlp, :]
        bz32[k] = part
        bz[k] = part.astype(BF16)
    bz_wait = send_all(bz, bz_r, Z, z, z_peer, bz_send, bz_recv)

    parts = hpart.at[pl.ds(0, Z - 1)]
    gz_wait = rcopy(parts, parts, gz_send, gz_recv, other_core)
    gz_wait.wait_recv()
    for k in range(Z):
        hpack[k * d.hz : k * d.hz + d.hzp, :] = hpart[k].astype(F32)
    hall[core, s] = hpack[0 : d.hx, :].astype(BF16)
    part = hall.at[core, s]
    for k in range(1, X):
        rcopy(part, part, gx_send, gx_recv, x_peer(k)).start()

    bz_wait.wait_recv()
    total = bz32[z]
    for k in range(Z - 1):
        total = total + bz_r[k].astype(F32)
    last(total, brow)
    parts = hall.at[core, pl.ds(0, X - 1)]
    gx_wait = rcopy(parts, parts, gx_send, gx_recv, other_core)
    gx_wait.wait_recv()
    gcore = rcopy(hall.at[core], hall.at[core], core_send.at[2], core_recv.at[2], other_core)
    gcore.start()

    total = jnp.zeros((d.hbp, 128), F32)
    pltpu.make_async_copy(ls, l_r, l_recv).wait()
    for k in range(Y):
        total = total + l_r[k].astype(F32)
    gconv_o[...] = total[0 : d.hb, :] * d.scale

    rcopy(
        hall.at[1 - core], hall.at[1 - core], core_send.at[2], core_recv.at[2], other_core
    ).wait_recv()
    for c in range(2):
        for x in range(X):
            at = c * d.hc + x * d.hx
            h32[at : at + d.hx, :] = hall[c, x].astype(F32)
    for half in range(d.head // C):
        gup_o[:, half * C : (half + 1) * C] = h32[half * C : (half + 1) * C, :] * d.scale
    for half in range(2):
        gout_o[half * depth : (half + 1) * depth, :] = (
            h32[base : base + depth, half * d.outc : (half + 1) * d.outc] * d.scale
        )

    parts = ret.at[all_but_one]
    b_wait = rcopy(parts, gcam_o.at[all_but_one], b_send, b_recv, other_core)
    b_wait.wait_recv()

    rcopy(parts, parts, a_send, a_recv, other_core).wait_send()
    b_wait.wait_send()
    for k in range(2):
        rcopy(rows_s.at[k], rows_r.at[k], row_send.at[k], row_recv.at[k], other_core).wait_send()
        rcopy(cols_r.at[k], cols_r.at[k], col_send.at[k], col_recv.at[k], other_core).wait_send()
    for wait in (
        bx_wait, bz_wait, hx_wait, hz_wait, hy_wait, gz_wait, gx_wait,
        core_copy, hcore_copy, gcore,
    ):
        wait.wait_send()

    @pl.when(self_group)
    def _():
        parts = ls.at[pl.ds(0, Y - 1)]
        rcopy(parts, parts, l_send, l_recv, other_core).wait_send()

    @pl.when(jnp.logical_not(self_group))
    def _():
        rcopy(ls, ls, l_send, l_recv, other_core).wait_send()

    own_out.wait()


def copy_kernel(*refs):
    stores = [
        pltpu.make_async_copy(refs[k], refs[6 + k], refs[12].at[k]) for k in range(6)
    ]
    for store in stores:
        store.start()
    for store in stores:
        store.wait()


def per_device(
    cam_send, lidar_bev, tile_active, tile_source, conv_weight, head_up, head_out, cotangent
):
    channels = cam_send.shape[5]
    cells_x, cells_y = lidar_bev.shape[1], lidar_bev.shape[2]
    head, outc = head_out.shape
    d = Dims(
        lax.axis_size("src"), lax.axis_size("gx"), lax.axis_size("gy"),
        cells_x, cells_y, channels, head, outc,
    )
    C, X, Y, Z, N = d.c, d.X, d.Y, d.Z, d.N
    cells = d.cells
    vmem = pl.BlockSpec(memory_space=pltpu.VMEM)
    anyw = pl.BlockSpec(memory_space=pl.ANY)
    dma = pltpu.SemaphoreType.DMA

    def b16(*shape):
        return pltpu.VMEM(shape, BF16)

    def f32(*shape):
        return pltpu.VMEM(shape, F32)

    def i32(*shape):
        return pltpu.VMEM(shape, jnp.int32)

    scratch = [
        b16(N, 2, 16, C), b16(cells, C), b16(3, 3 * C, C), b16(C, head), b16(head, outc),
        b16(cells, outc), i32(d.tx, d.ty), i32(d.tx, d.ty), pltpu.SMEM((d.tx, d.ty), jnp.int32),
        i32(8, 128), pltpu.SMEM((8, 128), jnp.int32),
        b16(3, 3 * C, C), b16(head, C), b16(outc, head), f32(d.tx, cells_y, C),
        f32(cells_x, cells_y, C), f32(cells_x, cells_y, C),
        b16((cells_x + 2) * cells_y, 3 * C), b16((cells_x + 2) * cells_y, 3 * C),
        b16(2, 2, cells_y, C), b16(2, 2, cells_y, C),
        b16(2, 2, d.colp, C), b16(2, 2, 3, d.colp, C),
        b16(cells, C), b16(cells, head), b16(cells, head), b16(cells, C),
        b16(d.tiles, 16, C), b16(N, 2, 16, C),
        f32(d.rows, C), b16(d.rows, C), b16(d.rc, C), f32(d.rc, C),
        b16(X, d.bx, C), b16(X - 1, d.bx, C), f32(d.bx + d.rlp, C),
        f32(Z, d.rlp, C), b16(Z, d.rlp, C), b16(Z - 1, d.rlp, C), f32(2 * d.rlp + 16, 128),
        b16(Y, d.hbp, 128), b16(Y, d.hbp, 128),
        f32(d.hrows, C), b16(d.hrows, C), b16(d.hc, C), f32(d.hc, C),
        b16(X, d.hx, C), b16(X - 1, d.hx, C), f32(d.hx + 16, C),
        f32(Z, d.hzp, C), b16(Z, d.hzp, C), b16(Z - 1, d.hzp, C),
        b16(d.hzp, C), b16(Y - 1, d.hzp, C),
        b16(Z, d.hzp, C), f32(d.hx + 16, C), b16(2, X, d.hx, C),
        dma((9,)), dma,
        dma, dma, dma, dma, dma((2,)), dma((2,)), dma((2,)), dma((2,)), dma((3,)), dma((3,)),
        *[dma] * 16,
    ]
    results = pl.pallas_call(
        functools.partial(kernel, d),
        out_shape=(
            pltpu.VMEM((cells, outc), BF16),
            pltpu.VMEM((cells, C), BF16),
            pltpu.VMEM((N, 2, 16, C), BF16),
            pltpu.VMEM((d.hb, 128), F32),
            pltpu.VMEM((C, head), F32),
            pltpu.VMEM((head, outc), F32),
        ),
        in_specs=[anyw] * 8,
        out_specs=(vmem,) * 6,
        scratch_shapes=scratch,
        compiler_params=pltpu.CompilerParams(
            collective_id=0, has_side_effects=True, vmem_limit_bytes=VMEM_BYTES
        ),
    )(
        cam_send.reshape(N, 2, 16, C),
        lidar_bev.reshape(cells, C),
        tile_active.reshape(d.tx, d.ty),
        tile_source.reshape(d.tx, d.ty),
        conv_weight.reshape(3, 3 * C, C),
        head_up,
        head_out,
        cotangent.reshape(cells, outc),
    )
    maps, gin, gcam, gconv, gup, gout = pl.pallas_call(
        copy_kernel,
        out_shape=tuple(jax.ShapeDtypeStruct(a.shape, a.dtype) for a in results),
        in_specs=[vmem] * 6,
        out_specs=(anyw,) * 6,
        scratch_shapes=[dma((6,))],
        compiler_params=pltpu.CompilerParams(vmem_limit_bytes=1024 * 1024),
    )(*results)
    return (
        maps.reshape(1, cells_x, cells_y, outc),
        gin.reshape(1, cells_x, cells_y, C),
        gcam.reshape(1, 1, N, 2, 16, C),
        gconv.reshape(-1),
        gup,
        gout,
    )


def solution(mesh):
    in_specs = (
        P(("src", "gx"), "gy", None, None, None, None),
        P("src", "gx", "gy", None),
        P("src", "gx", "gy"),
        P("src", "gx", "gy"),
        P(),
        P(),
        P(),
        P("src", "gx", "gy", None),
    )
    out_specs = (
        P("src", "gx", "gy", None),
        P("src", "gx", "gy", None),
        P(("src", "gx"), "gy", None, None, None, None),
        P(("src", "gx", "gy")),
        P(),
        P(),
    )
    return jax.shard_map(
        per_device, mesh=mesh, in_specs=in_specs, out_specs=out_specs, check_vma=False
    )
```

```python
import functools
import math

import jax
import jax.numpy as jnp
from jax import lax
from jax.experimental import pallas as pl
from jax.experimental.pallas import tpu as pltpu
from jax.sharding import PartitionSpec as P

MESH = pl.DeviceIdType.MESH
F32 = jnp.float32
BF16 = jnp.bfloat16
VMEM_BYTES = (62 * 1024 - 256) * 1024


def pad16(rows):
    return (rows + 15) // 16 * 16


def sigmoid(value):
    return 0.5 * jnp.tanh(0.5 * value) + 0.5


def dot(lhs, rhs):
    return jnp.dot(lhs, rhs, preferred_element_type=F32)


def dot_tn(lhs, rhs):
    return lax.dot_general(lhs, rhs, (((0,), (0,)), ((), ())), preferred_element_type=F32)


def rcopy(src, dst, send_sem, recv_sem, device):
    return pltpu.make_async_remote_copy(
        src_ref=src,
        dst_ref=dst,
        send_sem=send_sem,
        recv_sem=recv_sem,
        device_id=device,
        device_id_type=MESH,
    )


class Dims:
    def __init__(self, n_src, n_gx, n_gy, cells_x, cells_y, channels, head, outc):
        self.X, self.GX, self.GY = n_src, n_gx, n_gy
        self.YL, self.Z, self.Y = n_gx // 2, n_gy // 2, n_gx
        self.N = n_src * n_gx
        self.cx, self.cy, self.c = cells_x, cells_y, channels
        self.cells = cells_x * cells_y
        self.tx, self.ty = cells_x // 4, cells_y // 4
        self.tiles = self.tx * self.ty
        self.head, self.outc = head, outc
        self.colp = pad16(cells_x)
        self.rows = 9 * channels
        self.rc = self.rows // 2
        self.units = n_src * self.YL
        self.u = self.rc // self.units
        self.up = pad16(self.u)
        self.uz = self.u // self.Z
        self.bx = self.rc // self.X
        self.rl = self.bx // self.Z
        self.rlp = pad16(self.rl)
        self.hb = 2 * self.rl // self.Y
        self.hbp = pad16(self.hb)
        self.hrows = (channels * head + head * outc) // channels
        self.hc = self.hrows // 2
        self.hx = self.hc // self.X
        self.hz = self.hx // self.Z
        self.hzp = pad16(self.hz)
        self.scale = 1.0 / math.sqrt(n_src * n_gx * n_gy * cells_x * cells_y)


def kernel(
    d,
    cam, lidar_h, act_h, tsrc_h, wconv_h, hup_h, hout_h, cot_h,
    maps_o, gin_o, gcam_o, gconv_o, gup_o, gout_o,
    arrived, lidar, wconv, hup, hout, cot, act, tvec, tsrc, inv_v, inv,
    wt, hup_t, hout_t, mask,
    m32, conv, m3, g3, rows_s, rows_r, cols_s, cols_r,
    feat, hid, gh, gp, tiles, ret,
    dw32, dwb, core_r, cs32,
    bx, bx_r, bxsum, bz32, bz, bz_r, brow, l32, ls, l_r,
    h32, hb, hcore_r, hs32, hxs, hx_r, hxsum, hzs32, hzs, hz_r, hy, hy_r, hpart, hpack, hall,
    in_sem, out_sem,
    a_send, a_recv, b_send, b_recv, row_send, row_recv, col_send, col_recv, core_send, core_recv,
    bx_send, bx_recv, bz_send, bz_recv, l_send, l_recv,
    hx_send, hx_recv, hz_send, hz_recv, hy_send, hy_recv, gz_send, gz_recv, gx_send, gx_recv,
):
    s = lax.axis_index("src")
    g = lax.axis_index("gx")
    r = lax.axis_index("gy")
    core, yl = g % 2, g // 2
    z, yh = r // 2, r % 2
    me = s * d.GX + g
    X, Y, Z, N, C, CY = d.X, d.Y, d.Z, d.N, d.c, d.cy

    loads = [
        pltpu.make_async_copy(src, dst, in_sem.at[k])
        for k, (src, dst) in enumerate(
            [(act_h, act), (tsrc_h, tvec), (tsrc_h, tsrc), (wconv_h, wconv), (hup_h, hup),
             (hout_h, hout), (lidar_h, lidar), (cot_h, cot), (cam.at[me], arrived.at[me])]
        )
    ]

    order = (3, 2, 1, 0) if d.YL == 4 else range(d.YL - 1, -1, -1)

    def a_peer(far, step):
        to_s = (s + step // 2) % X
        if d.YL == 4:
            to_yl = {3: 3 - yl, 2: (yl + 2) % 4, 1: yl + 1 - 2 * (yl % 2), 0: yl}[far]
        else:
            to_yl = (yl + far) % d.YL
        to_g = to_yl * 2 + (core + step) % 2
        return to_s * d.GX + to_g, (to_s, to_g, r)

    def each_peer(body):
        for far in order:
            if far:
                body(far, 0)

        def rest(step, _):
            for far in order:
                body(far, step)
            return 0

        lax.fori_loop(1, 2 * X, rest, 0)

    def z_peer(step):
        return (s, g, ((z + step) % Z) * 2 + yh)

    def x_peer(step):
        return ((s + step) % X, g, r)

    def y_peer(step):
        at = (yl * 2 + yh + step) % Y
        return (s, (at // 2) * 2 + core, z * 2 + at % 2)

    other_core = (s, yl * 2 + 1 - core, r)

    my_y = yl * 2 + yh

    barrier = pltpu.get_barrier_semaphore()

    def greet(device):
        pl.semaphore_signal(barrier, inc=1, device_id=device, device_id_type=MESH)

    each_peer(lambda far, step: greet(a_peer(far, step)[1]))
    count = N - 1
    for step in range(1, Z):
        greet(z_peer(step))
        count += 1
    for at in range(d.YL):
        greet((s, at * 2 + core, z * 2 + 1 - yh))
        count += 1
    for side in (-1, 1):
        for near in (-1, 0, 1):
            greet((s, (g + near + d.GX) % d.GX, (r + side + d.GY) % d.GY))
            count += 1
    pl.semaphore_wait(barrier, count)

    def a_start(far, step):
        to, device = a_peer(far, step)
        rcopy(cam.at[to], arrived.at[me], a_send, a_recv, device).start()

    each_peer(a_start)
    for load in loads:
        load.start()

    for load in loads[:6]:
        load.wait()
    at_y = lax.broadcasted_iota(jnp.int32, (CY, d.ty), 0) // 4
    at_q = lax.broadcasted_iota(jnp.int32, (CY, d.ty), 1)
    for p in range(d.tx):
        row = act[p : p + 1, :].astype(F32)
        column = jnp.sum(jnp.where(at_y == at_q, row, 0.0), axis=1, keepdims=True)
        mask[p] = jnp.broadcast_to(column, (CY, C))
    eye = lax.broadcasted_iota(jnp.int32, (d.ty, d.ty), 0) == lax.broadcasted_iota(
        jnp.int32, (d.ty, d.ty), 1
    )
    at_t = lax.broadcasted_iota(jnp.int32, (d.ty, 128), 0)
    at_s = lax.broadcasted_iota(jnp.int32, (d.ty, 128), 1)
    found = jnp.zeros((1, 128), jnp.int32)
    for p in range(d.tx):
        column = jnp.sum(jnp.where(eye, tvec[p : p + 1, :], 0), axis=1, keepdims=True)
        hit = jnp.where(column == at_s, at_t + p * d.ty, 0)
        found = jnp.maximum(found, jnp.max(hit, axis=0, keepdims=True))
    inv_v[...] = jnp.broadcast_to(found, (8, 128))
    inv_copy = pltpu.make_async_copy(inv_v, inv, in_sem.at[0])
    inv_copy.start()
    for i in range(3):
        for j in range(3):
            tap = wconv[2 - i, (2 - j) * C : (3 - j) * C, :].astype(F32)
            wt[i, j * C : (j + 1) * C, :] = tap.T.astype(BF16)
    hup_t[...] = hup[...].astype(F32).T.astype(BF16)
    hout_t[...] = hout[...].astype(F32).T.astype(BF16)

    inv_copy.wait()
    for load in loads[6:]:
        load.wait()
    all_but_one = pl.ds(0, N - 1)
    rcopy(
        arrived.at[all_but_one], arrived.at[all_but_one], a_send, a_recv, other_core
    ).wait_recv()

    span = 4 * CY

    def merge(p, _):
        for q in range(d.ty):
            at = tsrc[p, q]
            tile = arrived[at // 2, at % 2].astype(F32)
            for dx in range(4):
                m32[4 * p + dx, 4 * q : 4 * q + 4, :] = tile[4 * dx : 4 * dx + 4]
        for dx in range(4):
            x = 4 * p + dx
            line = pl.ds(pl.multiple_of(x * CY, CY), CY)
            m32[x] = mask[p] * (m32[x] + lidar[line, :].astype(F32))
        return 0

    lax.fori_loop(0, d.tx, merge, 0)

    def send_all(parts, slots, size, here, peer, send_sem, recv_sem):
        for k in range(1, size):
            rcopy(parts.at[(here + k) % size], slots.at[k - 1], send_sem, recv_sem, peer(k)).start()
        return rcopy(slots, slots, send_sem, recv_sem, other_core)

    def halo_start(k):
        rows_s[k, 0] = m32[0].astype(BF16)
        rows_s[k, 1] = m32[d.cx - 1].astype(BF16)
        cols_s[k, 0, 0 : d.cx, :] = m32[:, 0, :].astype(BF16)
        cols_s[k, 1, 0 : d.cx, :] = m32[:, CY - 1, :].astype(BF16)
        for side, step in ((0, -1), (1, 1)):
            for near in (-1, 0, 1):
                device = (s, (g + near + d.GX) % d.GX, (r + step + d.GY) % d.GY)
                rcopy(
                    cols_s.at[k, side], cols_r.at[k, 1 - side, 1 - near], col_send.at[k],
                    col_recv.at[k], device,
                ).start()
            device = (s, (g + step + d.GX) % d.GX, r)
            rcopy(
                rows_s.at[k, side], rows_r.at[k, 1 - side], row_send.at[k], row_recv.at[k], device
            ).start()

    at_row = lax.broadcasted_iota(jnp.int32, (CY, C), 0)
    head_row = lax.broadcasted_iota(jnp.int32, (16, C), 0)

    def put(out3, x, line, left, right):
        down = jnp.where(at_row == 0, left, pltpu.roll(line, 1, 0))
        up = jnp.where(at_row == CY - 1, right, pltpu.roll(line, CY - 1, 0))
        out3[x * CY : (x + 1) * CY, 0:C] = down.astype(BF16)
        out3[x * CY : (x + 1) * CY, C : 2 * C] = line.astype(BF16)
        out3[x * CY : (x + 1) * CY, 2 * C : 3 * C] = up.astype(BF16)

    def put_ends(out3, x, left, right):
        top = m32[x - 1, 0:16, :]
        low = m32[x - 1, CY - 16 : CY, :]
        down = jnp.where(head_row == 0, left, pltpu.roll(top, 1, 0))
        up = jnp.where(head_row == 15, right, pltpu.roll(low, 15, 0))
        out3[x * CY : x * CY + 16, 0:C] = down.astype(BF16)
        out3[(x + 1) * CY - 16 : (x + 1) * CY, 2 * C : 3 * C] = up.astype(BF16)

    def halo_inner(out3):
        for x in range(d.cx):
            put(out3, x + 1, m32[x], 0.0, 0.0)

    def halo_finish(k, out3, ends):
        rcopy(rows_s.at[k], rows_r.at[k], row_send.at[k], row_recv.at[k], other_core).wait_recv()
        rcopy(cols_r.at[k], cols_r.at[k], col_send.at[k], col_recv.at[k], other_core).wait_recv()
        ok_g = (g > 0, g < d.GX - 1)
        ok_r = (r > 0, r < d.GY - 1)
        lefts = [jnp.where(ok_r[0], cols_r[k, 0, near].astype(F32), 0.0) for near in range(3)]
        rights = [jnp.where(ok_r[1], cols_r[k, 1, near].astype(F32), 0.0) for near in range(3)]
        for side, x, row in ((0, 0, d.cx - 1), (1, d.cx + 1, 0)):
            line = rows_r[k, side].astype(F32)
            near = 0 if side == 0 else 2
            line, left, right = [
                jnp.where(ok_g[side], value, 0.0)
                for value in (line, lefts[near][row : row + 1], rights[near][row : row + 1])
            ]
            put(out3, x, line, left, right)
        for x in range(d.cx):
            left, right = lefts[1][x : x + 1], rights[1][x : x + 1]
            if ends:
                put_ends(out3, x + 1, left, right)

    def conv_inner(from3, weight):
        from3[0:CY, :] = jnp.zeros((CY, 3 * C), BF16)
        from3[(d.cx + 1) * CY :, :] = jnp.zeros((CY, 3 * C), BF16)

        def chunk(p, _):
            acc = jnp.zeros((span, C), F32)
            for i in range(3):
                start = pl.multiple_of(p * span + i * CY, CY)
                acc = acc + dot(from3[pl.ds(start, span), :], weight[i])
            conv[pl.ds(4 * p, 4)] = acc.reshape(4, CY, C)
            return 0

        lax.fori_loop(0, d.tx, chunk, 0, unroll=True)

    def conv_edges(k, from3, weight):
        conv[0] = conv[0] + dot(from3[0:CY, :], weight[0])
        conv[d.cx - 1] = conv[d.cx - 1] + dot(from3[(d.cx + 1) * CY :, :], weight[2])
        at = lax.broadcasted_iota(jnp.int32, (d.colp, C), 0)
        for side, y, ok in ((0, 0, r > 0), (1, CY - 1, r < d.GY - 1)):
            line = cols_r[k, side, 1].astype(F32)
            line = jnp.where(jnp.logical_and(ok, at < d.cx), line, 0.0).astype(BF16)
            tap = 2 * side
            before, here, after = [
                dot(line, weight[i, tap * C : (tap + 1) * C, :]) for i in range(3)
            ]
            before = jnp.where(at == 0, 0.0, pltpu.roll(before, 1, 0))
            after = jnp.where(at == d.colp - 1, 0.0, pltpu.roll(after, d.colp - 1, 0))
            total = before + here + after
            conv[:, y, :] = conv[:, y, :] + total[0 : d.cx]

    halo_start(0)
    halo_inner(m3)
    conv_inner(m3, wconv)
    halo_finish(0, m3, True)
    conv_edges(0, m3, wconv)

    def forward(p, _):
        here = pl.ds(pl.multiple_of(p * span, span), span)
        pre = conv[pl.ds(4 * p, 4)].reshape(span, C)
        occupied = jnp.concatenate([mask[p]] * 4, axis=0)
        sig = sigmoid(pre)
        feature = (occupied * (pre * sig)).astype(BF16)
        slope = occupied * (sig * (1.0 + pre * (1.0 - sig)))
        feat[here, :] = feature
        lines = pl.ds(4 * p, 4)
        m32[lines] = slope.reshape(4, CY, C)
        up = dot(feature, hup[...])
        sig = sigmoid(up)
        hidden = (up * sig).astype(BF16)
        hid[here, :] = hidden
        maps_o[here, :] = dot(hidden, hout[...]).astype(BF16)
        grad = (dot(cot[here, :], hout_t[...]) * (sig * (1.0 + up * (1.0 - sig)))).astype(BF16)
        gh[here, :] = grad
        value = dot(grad, hup_t[...]) * m32[lines].reshape(span, C)
        m32[lines] = value.reshape(4, CY, C)
        gp[here, :] = value.astype(BF16)
        return 0

    lax.fori_loop(0, d.tx, forward, 0, unroll=True)
    halo_start(1)
    term = dot_tn(feat[...], gh[...])
    for half in range(d.head // C):
        h32[half * C : (half + 1) * C, :] = term[:, half * C : (half + 1) * C]
    base = d.head
    term = dot_tn(hid[...], cot[...])
    depth = d.head // 2
    for half in range(2):
        h32[base : base + depth, half * d.outc : (half + 1) * d.outc] = term[
            half * depth : (half + 1) * depth, :
        ]
    hb[...] = h32[...].astype(BF16)
    hmine = pl.ds(pl.multiple_of(core * d.hc, d.hc), d.hc)
    htheirs = pl.ds(pl.multiple_of((1 - core) * d.hc, d.hc), d.hc)
    hcore_copy = rcopy(hb.at[htheirs], hcore_r, core_send.at[1], core_recv.at[1], other_core)
    hcore_copy.start()

    def tap_grads(i, _):
        for j in range(3):
            term = dot_tn(
                m3[pl.ds(pl.multiple_of(i * CY, CY), d.cells), j * C : (j + 1) * C], gp[...]
            )
            at = pl.ds(pl.multiple_of(i * (3 * C) + j * C, C), C)
            dw32[at, :] = term
        return 0

    lax.fori_loop(0, 3, tap_grads, 0)
    for k in range(d.units):
        theirs = pl.ds(pl.multiple_of((2 * k + 1 - core) * d.u, 8), d.u)
        dwb[k, 0 : d.u, :] = dw32[theirs, :].astype(BF16)
    core_copy = rcopy(dwb, core_r, core_send.at[0], core_recv.at[0], other_core)
    core_copy.start()

    hcore_copy.wait_recv()
    hs32[...] = h32[hmine, :] + hcore_r[...].astype(F32)
    for k in range(X):
        hxs[k] = hs32[k * d.hx : (k + 1) * d.hx, :].astype(BF16)
    hx_wait = send_all(hxs, hx_r, X, s, x_peer, hx_send, hx_recv)

    halo_inner(g3)
    conv_inner(g3, wt)

    hx_wait.wait_recv()
    total = hs32[pl.ds(pl.multiple_of(s * d.hx, d.hx), d.hx), :]
    for k in range(X - 1):
        total = total + hx_r[k].astype(F32)
    hxsum[0 : d.hx, :] = total
    for k in range(Z):
        part = hxsum[k * d.hz : k * d.hz + d.hzp, :]
        hzs32[k] = part
        hzs[k] = part.astype(BF16)
    hz_wait = send_all(hzs, hz_r, Z, z, z_peer, hz_send, hz_recv)

    core_copy.wait_recv()
    for k in range(d.units):
        mine = pl.ds(pl.multiple_of((2 * k + core) * d.u, 8), d.u)
        cs32[k * d.u : (k + 1) * d.u, :] = dw32[mine, :] + core_r[k, 0 : d.u, :].astype(F32)
    for k in range(X):
        bx[k] = cs32[k * d.bx : (k + 1) * d.bx, :].astype(BF16)
    bx_wait = send_all(bx, bx_r, X, s, x_peer, bx_send, bx_recv)

    halo_finish(1, g3, False)
    conv_edges(1, g3, wt)

    def backward(p, _):
        here = pl.ds(pl.multiple_of(p * span, span), span)
        acc = conv[pl.ds(4 * p, 4)].reshape(span, C)
        acc = acc * jnp.concatenate([mask[p]] * 4, axis=0)
        gin_o[here, :] = acc.astype(BF16)
        m32[pl.ds(4 * p, 4)] = acc.reshape(4, CY, C)
        for q in range(d.ty):
            parts = [m32[4 * p + dx, 4 * q : 4 * q + 4, :] for dx in range(4)]
            tiles[p * d.ty + q] = jnp.concatenate(parts, axis=0).astype(BF16)
        return 0

    lax.fori_loop(0, d.tx, backward, 0, unroll=True)
    hz_wait.wait_recv()
    total = hzs32[z]
    for k in range(Z - 1):
        total = total + hz_r[k].astype(F32)
    hy[...] = total.astype(BF16)
    for k in range(1, Y):
        rcopy(hy, hy_r.at[k - 1], hy_send, hy_recv, y_peer(k)).start()
    hy_wait = rcopy(hy_r, hy_r, hy_send, hy_recv, other_core)

    def b_start(far, step):
        to, device = a_peer(far, step)
        for slot in range(2):
            ret[to, slot] = tiles[inv[0, to * 2 + slot]]
        rcopy(ret.at[to], gcam_o.at[me], b_send, b_recv, device).start()

    each_peer(b_start)
    for slot in range(2):
        ret[me, slot] = tiles[inv[0, me * 2 + slot]]
    own_out = pltpu.make_async_copy(ret.at[me], gcam_o.at[me], out_sem)
    own_out.start()

    hy_wait.wait_recv()
    total = hy[...].astype(F32)
    for k in range(Y - 1):
        total = total + hy_r[k].astype(F32)
    hpart[z] = total.astype(BF16)
    part = hpart.at[z]
    for k in range(1, Z):
        rcopy(part, part, gz_send, gz_recv, z_peer(k)).start()

    bx_wait.wait_recv()
    total = cs32[pl.ds(pl.multiple_of(s * d.bx, 8), d.bx), :]
    for k in range(X - 1):
        total = total + bx_r[k].astype(F32)
    bxsum[0 : d.bx, :] = total
    for k in range(Z):
        for y in range(d.YL):
            here = y * d.u + k * d.uz
            bz32[k, y * d.uz : (y + 1) * d.uz, :] = bxsum[here : here + d.uz, :]
        bz[k] = bz32[k].astype(BF16)
    bz_wait = send_all(bz, bz_r, Z, z, z_peer, bz_send, bz_recv)

    parts = hpart.at[pl.ds(0, Z - 1)]
    gz_wait = rcopy(parts, parts, gz_send, gz_recv, other_core)
    gz_wait.wait_recv()
    for k in range(Z):
        hpack[k * d.hz : k * d.hz + d.hzp, :] = hpart[k].astype(F32)
    hall[core, s] = hpack[0 : d.hx, :].astype(BF16)
    part = hall.at[core, s]
    for k in range(1, X):
        rcopy(part, part, gx_send, gx_recv, x_peer(k)).start()

    bz_wait.wait_recv()
    total = bz32[z]
    for k in range(Z - 1):
        total = total + bz_r[k].astype(F32)
    brow[pl.ds(0, d.rlp, stride=2), :] = total[:, 0:128]
    brow[pl.ds(1, d.rlp, stride=2), :] = total[:, 128:256]
    for k in range(Y):
        part = brow[k * d.hb : k * d.hb + d.hbp, :]
        l32[k] = part
        ls[k] = part.astype(BF16)
    l_wait = send_all(ls, l_r, Y, my_y, y_peer, l_send, l_recv)

    parts = hall.at[core, pl.ds(0, X - 1)]
    gx_wait = rcopy(parts, parts, gx_send, gx_recv, other_core)
    gx_wait.wait_recv()
    gcore = rcopy(hall.at[core], hall.at[core], core_send.at[2], core_recv.at[2], other_core)
    gcore.start()

    l_wait.wait_recv()
    total = l32[my_y]
    for k in range(Y - 1):
        total = total + l_r[k].astype(F32)
    gconv_o[...] = total[0 : d.hb, :] * d.scale

    rcopy(
        hall.at[1 - core], hall.at[1 - core], core_send.at[2], core_recv.at[2], other_core
    ).wait_recv()
    for c in range(2):
        for x in range(X):
            at = c * d.hc + x * d.hx
            h32[at : at + d.hx, :] = hall[c, x].astype(F32)
    for half in range(d.head // C):
        gup_o[:, half * C : (half + 1) * C] = h32[half * C : (half + 1) * C, :] * d.scale
    for half in range(2):
        gout_o[half * depth : (half + 1) * depth, :] = (
            h32[base : base + depth, half * d.outc : (half + 1) * d.outc] * d.scale
        )

    parts = ret.at[all_but_one]
    b_wait = rcopy(parts, gcam_o.at[all_but_one], b_send, b_recv, other_core)
    b_wait.wait_recv()

    rcopy(parts, parts, a_send, a_recv, other_core).wait_send()
    b_wait.wait_send()
    for k in range(2):
        rcopy(rows_s.at[k], rows_r.at[k], row_send.at[k], row_recv.at[k], other_core).wait_send()
        rcopy(cols_r.at[k], cols_r.at[k], col_send.at[k], col_recv.at[k], other_core).wait_send()
    for wait in (
        bx_wait, bz_wait, hx_wait, hz_wait, hy_wait, gz_wait, gx_wait,
        l_wait, core_copy, hcore_copy, gcore,
    ):
        wait.wait_send()

    own_out.wait()


def copy_kernel(*refs):
    stores = [
        pltpu.make_async_copy(refs[k], refs[6 + k], refs[12].at[k]) for k in range(6)
    ]
    for store in stores:
        store.start()
    for store in stores:
        store.wait()


def per_device(
    cam_send, lidar_bev, tile_active, tile_source, conv_weight, head_up, head_out, cotangent
):
    channels = cam_send.shape[5]
    cells_x, cells_y = lidar_bev.shape[1], lidar_bev.shape[2]
    head, outc = head_out.shape
    d = Dims(
        lax.axis_size("src"), lax.axis_size("gx"), lax.axis_size("gy"),
        cells_x, cells_y, channels, head, outc,
    )
    C, X, Y, Z, N = d.c, d.X, d.Y, d.Z, d.N
    cells = d.cells
    vmem = pl.BlockSpec(memory_space=pltpu.VMEM)
    anyw = pl.BlockSpec(memory_space=pl.ANY)
    dma = pltpu.SemaphoreType.DMA

    def b16(*shape):
        return pltpu.VMEM(shape, BF16)

    def f32(*shape):
        return pltpu.VMEM(shape, F32)

    def i32(*shape):
        return pltpu.VMEM(shape, jnp.int32)

    scratch = [
        b16(N, 2, 16, C), b16(cells, C), b16(3, 3 * C, C), b16(C, head), b16(head, outc),
        b16(cells, outc), i32(d.tx, d.ty), i32(d.tx, d.ty), pltpu.SMEM((d.tx, d.ty), jnp.int32),
        i32(8, 128), pltpu.SMEM((8, 128), jnp.int32),
        b16(3, 3 * C, C), b16(head, C), b16(outc, head), f32(d.tx, cells_y, C),
        f32(cells_x, cells_y, C), f32(cells_x, cells_y, C),
        b16((cells_x + 2) * cells_y, 3 * C), b16((cells_x + 2) * cells_y, 3 * C),
        b16(2, 2, cells_y, C), b16(2, 2, cells_y, C),
        b16(2, 2, d.colp, C), b16(2, 2, 3, d.colp, C),
        b16(cells, C), b16(cells, head), b16(cells, head), b16(cells, C),
        b16(d.tiles, 16, C), b16(N, 2, 16, C),
        f32(d.rows, C), b16(d.units, d.up, C), b16(d.units, d.up, C), f32(d.rc, C),
        b16(X, d.bx, C), b16(X - 1, d.bx, C), f32(d.bx + d.rlp, C),
        f32(Z, d.rlp, C), b16(Z, d.rlp, C), b16(Z - 1, d.rlp, C), f32(2 * d.rlp + 16, 128),
        f32(Y, d.hbp, 128), b16(Y, d.hbp, 128), b16(Y - 1, d.hbp, 128),
        f32(d.hrows, C), b16(d.hrows, C), b16(d.hc, C), f32(d.hc, C),
        b16(X, d.hx, C), b16(X - 1, d.hx, C), f32(d.hx + 16, C),
        f32(Z, d.hzp, C), b16(Z, d.hzp, C), b16(Z - 1, d.hzp, C),
        b16(d.hzp, C), b16(Y - 1, d.hzp, C),
        b16(Z, d.hzp, C), f32(d.hx + 16, C), b16(2, X, d.hx, C),
        dma((9,)), dma,
        dma, dma, dma, dma, dma((2,)), dma((2,)), dma((2,)), dma((2,)), dma((3,)), dma((3,)),
        *[dma] * 16,
    ]
    results = pl.pallas_call(
        functools.partial(kernel, d),
        out_shape=(
            pltpu.VMEM((cells, outc), BF16),
            pltpu.VMEM((cells, C), BF16),
            pltpu.VMEM((N, 2, 16, C), BF16),
            pltpu.VMEM((d.hb, 128), F32),
            pltpu.VMEM((C, head), F32),
            pltpu.VMEM((head, outc), F32),
        ),
        in_specs=[anyw] * 8,
        out_specs=(vmem,) * 6,
        scratch_shapes=scratch,
        compiler_params=pltpu.CompilerParams(
            collective_id=0, has_side_effects=True, vmem_limit_bytes=VMEM_BYTES
        ),
    )(
        cam_send.reshape(N, 2, 16, C),
        lidar_bev.reshape(cells, C),
        tile_active.reshape(d.tx, d.ty),
        tile_source.reshape(d.tx, d.ty),
        conv_weight.reshape(3, 3 * C, C),
        head_up,
        head_out,
        cotangent.reshape(cells, outc),
    )
    maps, gin, gcam, gconv, gup, gout = pl.pallas_call(
        copy_kernel,
        out_shape=tuple(jax.ShapeDtypeStruct(a.shape, a.dtype) for a in results),
        in_specs=[vmem] * 6,
        out_specs=(anyw,) * 6,
        scratch_shapes=[dma((6,))],
        compiler_params=pltpu.CompilerParams(vmem_limit_bytes=1024 * 1024),
    )(*results)
    return (
        maps.reshape(1, cells_x, cells_y, outc),
        gin.reshape(1, cells_x, cells_y, C),
        gcam.reshape(1, 1, N, 2, 16, C),
        gconv.reshape(-1),
        gup,
        gout,
    )


def solution(mesh):
    in_specs = (
        P(("src", "gx"), "gy", None, None, None, None),
        P("src", "gx", "gy", None),
        P("src", "gx", "gy"),
        P("src", "gx", "gy"),
        P(),
        P(),
        P(),
        P("src", "gx", "gy", None),
    )
    out_specs = (
        P("src", "gx", "gy", None),
        P("src", "gx", "gy", None),
        P(("src", "gx"), "gy", None, None, None, None),
        P(("src", "gx", "gy")),
        P(),
        P(),
    )
    return jax.shard_map(
        per_device, mesh=mesh, in_specs=in_specs, out_specs=out_specs, check_vma=False
    )
```

```python
import functools
import math

import jax
import jax.numpy as jnp
from jax import lax
from jax.experimental import pallas as pl
from jax.experimental.pallas import tpu as pltpu
from jax.sharding import PartitionSpec as P

MESH = pl.DeviceIdType.MESH
F32 = jnp.float32
BF16 = jnp.bfloat16
VMEM_BYTES = (62 * 1024 - 256) * 1024


def pad16(rows):
    return (rows + 15) // 16 * 16


def sigmoid(value):
    return 0.5 * jnp.tanh(0.5 * value) + 0.5


def dot(lhs, rhs):
    return jnp.dot(lhs, rhs, preferred_element_type=F32)


def dot_tn(lhs, rhs):
    return lax.dot_general(lhs, rhs, (((0,), (0,)), ((), ())), preferred_element_type=F32)


def rcopy(src, dst, send_sem, recv_sem, device):
    return pltpu.make_async_remote_copy(
        src_ref=src,
        dst_ref=dst,
        send_sem=send_sem,
        recv_sem=recv_sem,
        device_id=device,
        device_id_type=MESH,
    )


class Dims:
    def __init__(self, n_src, n_gx, n_gy, cells_x, cells_y, channels, head, outc):
        self.X, self.GX, self.GY = n_src, n_gx, n_gy
        self.YL, self.Z, self.Y = n_gx // 2, n_gy // 2, n_gx
        self.N = n_src * n_gx
        self.cx, self.cy, self.c = cells_x, cells_y, channels
        self.cells = cells_x * cells_y
        self.tx, self.ty = cells_x // 4, cells_y // 4
        self.tiles = self.tx * self.ty
        self.head, self.outc = head, outc
        self.colp = pad16(cells_x)
        self.rows = 9 * channels
        self.rc = self.rows // 2
        self.units = n_src * self.YL
        self.u = self.rc // self.units
        self.up = pad16(self.u)
        self.uz = self.u // self.Z
        self.bx = self.rc // self.X
        self.rl = self.bx // self.Z
        self.rlp = pad16(self.rl)
        self.hb = 2 * self.rl // self.Y
        self.hbp = pad16(self.hb)
        self.hrows = (channels * head + head * outc) // channels
        self.hc = self.hrows // 2
        self.hx = self.hc // self.X
        self.hz = self.hx // self.Z
        self.hzp = pad16(self.hz)
        self.scale = 1.0 / math.sqrt(n_src * n_gx * n_gy * cells_x * cells_y)


def kernel(
    d,
    cam, lidar_h, act_h, tsrc_h, wconv_h, hup_h, hout_h, cot_h,
    maps_o, gin_o, gcam_o, gconv_o, gup_o, gout_o,
    arrived, lidar, wconv, hup, hout, cot, act, tvec, tsrc, inv_v, inv,
    wt, hup_t, hout_t, mask,
    m32, conv, m3, g3, rows_s, rows_r, cols_s, cols_r,
    feat, hid, gh, gp, tiles, ret,
    dw32, dwb, core_r, cs32,
    bx, bx_r, bxsum, bz32, bz, bz_r, brow, l32, ls, l_r,
    h32, hb, hcore_r, hs32, hxs, hx_r, hxsum, hzs32, hzs, hz_r, hy, hy_r, hpart, hpack, hall,
    in_sem, out_sem,
    a_send, a_recv, b_send, b_recv, row_send, row_recv, col_send, col_recv, core_send, core_recv,
    bx_send, bx_recv, bz_send, bz_recv, l_send, l_recv,
    hx_send, hx_recv, hz_send, hz_recv, hy_send, hy_recv, gz_send, gz_recv, gx_send, gx_recv,
):
    s = lax.axis_index("src")
    g = lax.axis_index("gx")
    r = lax.axis_index("gy")
    core, yl = g % 2, g // 2
    z, yh = r // 2, r % 2
    me = s * d.GX + g
    X, Y, Z, N, C, CY = d.X, d.Y, d.Z, d.N, d.c, d.cy

    loads = [
        pltpu.make_async_copy(src, dst, in_sem.at[k])
        for k, (src, dst) in enumerate(
            [(act_h, act), (tsrc_h, tvec), (tsrc_h, tsrc), (wconv_h, wconv), (hup_h, hup),
             (hout_h, hout), (lidar_h, lidar), (cot_h, cot), (cam.at[me], arrived.at[me])]
        )
    ]

    order = (3, 2, 1, 0) if d.YL == 4 else range(d.YL - 1, -1, -1)

    def a_peer(far, step):
        to_s = (s + step // 2) % X
        if d.YL == 4:
            to_yl = {3: 3 - yl, 2: (yl + 2) % 4, 1: yl + 1 - 2 * (yl % 2), 0: yl}[far]
        else:
            to_yl = (yl + far) % d.YL
        to_g = to_yl * 2 + (core + step) % 2
        return to_s * d.GX + to_g, (to_s, to_g, r)

    def each_peer(body):
        for far in order:
            if far:
                body(far, 0)

        def rest(step, _):
            for far in order:
                body(far, step)
            return 0

        lax.fori_loop(1, 2 * X, rest, 0)

    def z_peer(step):
        return (s, g, ((z + step) % Z) * 2 + yh)

    def x_peer(step):
        return ((s + step) % X, g, r)

    def y_peer(step):
        at = (yl * 2 + yh + step) % Y
        return (s, (at // 2) * 2 + core, z * 2 + at % 2)

    other_core = (s, yl * 2 + 1 - core, r)

    my_y = yl * 2 + yh

    barrier = pltpu.get_barrier_semaphore()

    def greet(device):
        pl.semaphore_signal(barrier, inc=1, device_id=device, device_id_type=MESH)

    each_peer(lambda far, step: greet(a_peer(far, step)[1]))
    count = N - 1
    for step in range(1, Z):
        greet(z_peer(step))
        count += 1
    for at in range(d.YL):
        greet((s, at * 2 + core, z * 2 + 1 - yh))
        count += 1
    for side in (-1, 1):
        for near in (-1, 0, 1):
            greet((s, (g + near + d.GX) % d.GX, (r + side + d.GY) % d.GY))
            count += 1
    pl.semaphore_wait(barrier, count)

    def a_start(far, step):
        to, device = a_peer(far, step)
        rcopy(cam.at[to], arrived.at[me], a_send, a_recv, device).start()

    each_peer(a_start)
    for load in loads:
        load.start()

    for load in loads[:6]:
        load.wait()
    at_y = lax.broadcasted_iota(jnp.int32, (CY, d.ty), 0) // 4
    at_q = lax.broadcasted_iota(jnp.int32, (CY, d.ty), 1)
    for p in range(d.tx):
        row = act[p : p + 1, :].astype(F32)
        column = jnp.sum(jnp.where(at_y == at_q, row, 0.0), axis=1, keepdims=True)
        mask[p] = jnp.broadcast_to(column, (CY, C))
    eye = lax.broadcasted_iota(jnp.int32, (d.ty, d.ty), 0) == lax.broadcasted_iota(
        jnp.int32, (d.ty, d.ty), 1
    )
    at_t = lax.broadcasted_iota(jnp.int32, (d.ty, 128), 0)
    at_s = lax.broadcasted_iota(jnp.int32, (d.ty, 128), 1)
    found = jnp.zeros((1, 128), jnp.int32)
    for p in range(d.tx):
        column = jnp.sum(jnp.where(eye, tvec[p : p + 1, :], 0), axis=1, keepdims=True)
        hit = jnp.where(column == at_s, at_t + p * d.ty, 0)
        found = jnp.maximum(found, jnp.max(hit, axis=0, keepdims=True))
    inv_v[...] = jnp.broadcast_to(found, (8, 128))
    inv_copy = pltpu.make_async_copy(inv_v, inv, in_sem.at[0])
    inv_copy.start()
    for i in range(3):
        for j in range(3):
            tap = wconv[2 - i, (2 - j) * C : (3 - j) * C, :].astype(F32)
            wt[i, j * C : (j + 1) * C, :] = tap.T.astype(BF16)
    hup_t[...] = hup[...].astype(F32).T.astype(BF16)
    hout_t[...] = hout[...].astype(F32).T.astype(BF16)

    inv_copy.wait()
    for load in loads[6:]:
        load.wait()
    all_but_one = pl.ds(0, N - 1)
    rcopy(
        arrived.at[all_but_one], arrived.at[all_but_one], a_send, a_recv, other_core
    ).wait_recv()

    span = 4 * CY

    def merge(p, _):
        for q in range(d.ty):
            at = tsrc[p, q]
            tile = arrived[at // 2, at % 2].astype(F32)
            for dx in range(4):
                m32[4 * p + dx, 4 * q : 4 * q + 4, :] = tile[4 * dx : 4 * dx + 4]
        for dx in range(4):
            x = 4 * p + dx
            line = pl.ds(pl.multiple_of(x * CY, CY), CY)
            m32[x] = mask[p] * (m32[x] + lidar[line, :].astype(F32))
        return 0

    lax.fori_loop(0, d.tx, merge, 0)

    def send_all(parts, slots, size, here, peer, send_sem, recv_sem):
        for k in range(1, size):
            rcopy(parts.at[(here + k) % size], slots.at[k - 1], send_sem, recv_sem, peer(k)).start()
        return rcopy(slots, slots, send_sem, recv_sem, other_core)

    def halo_start(k):
        rows_s[k, 0] = m32[0].astype(BF16)
        rows_s[k, 1] = m32[d.cx - 1].astype(BF16)
        cols_s[k, 0, 0 : d.cx, :] = m32[:, 0, :].astype(BF16)
        cols_s[k, 1, 0 : d.cx, :] = m32[:, CY - 1, :].astype(BF16)
        for side, step in ((0, -1), (1, 1)):
            for near in (-1, 0, 1):
                device = (s, (g + near + d.GX) % d.GX, (r + step + d.GY) % d.GY)
                rcopy(
                    cols_s.at[k, side], cols_r.at[k, 1 - side, 1 - near], col_send.at[k],
                    col_recv.at[k], device,
                ).start()
            device = (s, (g + step + d.GX) % d.GX, r)
            rcopy(
                rows_s.at[k, side], rows_r.at[k, 1 - side], row_send.at[k], row_recv.at[k], device
            ).start()

    at_row = lax.broadcasted_iota(jnp.int32, (CY, C), 0)
    head_row = lax.broadcasted_iota(jnp.int32, (16, C), 0)

    def put(out3, x, line, left, right):
        down = jnp.where(at_row == 0, left, pltpu.roll(line, 1, 0))
        up = jnp.where(at_row == CY - 1, right, pltpu.roll(line, CY - 1, 0))
        out3[x * CY : (x + 1) * CY, 0:C] = down.astype(BF16)
        out3[x * CY : (x + 1) * CY, C : 2 * C] = line.astype(BF16)
        out3[x * CY : (x + 1) * CY, 2 * C : 3 * C] = up.astype(BF16)

    def put_ends(out3, x, left, right):
        top = m32[x - 1, 0:16, :]
        low = m32[x - 1, CY - 16 : CY, :]
        down = jnp.where(head_row == 0, left, pltpu.roll(top, 1, 0))
        up = jnp.where(head_row == 15, right, pltpu.roll(low, 15, 0))
        out3[x * CY : x * CY + 16, 0:C] = down.astype(BF16)
        out3[(x + 1) * CY - 16 : (x + 1) * CY, 2 * C : 3 * C] = up.astype(BF16)

    def halo_inner(out3):
        for x in range(d.cx):
            put(out3, x + 1, m32[x], 0.0, 0.0)

    def halo_finish(k, out3, ends):
        rcopy(rows_s.at[k], rows_r.at[k], row_send.at[k], row_recv.at[k], other_core).wait_recv()
        rcopy(cols_r.at[k], cols_r.at[k], col_send.at[k], col_recv.at[k], other_core).wait_recv()
        ok_g = (g > 0, g < d.GX - 1)
        ok_r = (r > 0, r < d.GY - 1)
        lefts = [jnp.where(ok_r[0], cols_r[k, 0, near].astype(F32), 0.0) for near in range(3)]
        rights = [jnp.where(ok_r[1], cols_r[k, 1, near].astype(F32), 0.0) for near in range(3)]
        for side, x, row in ((0, 0, d.cx - 1), (1, d.cx + 1, 0)):
            line = rows_r[k, side].astype(F32)
            near = 0 if side == 0 else 2
            line, left, right = [
                jnp.where(ok_g[side], value, 0.0)
                for value in (line, lefts[near][row : row + 1], rights[near][row : row + 1])
            ]
            put(out3, x, line, left, right)
        for x in range(d.cx):
            left, right = lefts[1][x : x + 1], rights[1][x : x + 1]
            if ends:
                put_ends(out3, x + 1, left, right)

    def conv_inner(from3, weight):
        from3[0:CY, :] = jnp.zeros((CY, 3 * C), BF16)
        from3[(d.cx + 1) * CY :, :] = jnp.zeros((CY, 3 * C), BF16)

        def chunk(p, _):
            acc = jnp.zeros((span, C), F32)
            for i in range(3):
                start = pl.multiple_of(p * span + i * CY, CY)
                acc = acc + dot(from3[pl.ds(start, span), :], weight[i])
            conv[pl.ds(4 * p, 4)] = acc.reshape(4, CY, C)
            return 0

        lax.fori_loop(0, d.tx, chunk, 0, unroll=True)

    def conv_edges(k, from3, weight):
        conv[0] = conv[0] + dot(from3[0:CY, :], weight[0])
        conv[d.cx - 1] = conv[d.cx - 1] + dot(from3[(d.cx + 1) * CY :, :], weight[2])
        at = lax.broadcasted_iota(jnp.int32, (d.colp, C), 0)
        for side, y, ok in ((0, 0, r > 0), (1, CY - 1, r < d.GY - 1)):
            line = cols_r[k, side, 1].astype(F32)
            line = jnp.where(jnp.logical_and(ok, at < d.cx), line, 0.0).astype(BF16)
            tap = 2 * side
            before, here, after = [
                dot(line, weight[i, tap * C : (tap + 1) * C, :]) for i in range(3)
            ]
            before = jnp.where(at == 0, 0.0, pltpu.roll(before, 1, 0))
            after = jnp.where(at == d.colp - 1, 0.0, pltpu.roll(after, d.colp - 1, 0))
            total = before + here + after
            conv[:, y, :] = conv[:, y, :] + total[0 : d.cx]

    halo_start(0)
    halo_inner(m3)
    conv_inner(m3, wconv)
    halo_finish(0, m3, True)
    conv_edges(0, m3, wconv)

    def forward(p, _):
        here = pl.ds(pl.multiple_of(p * span, span), span)
        pre = conv[pl.ds(4 * p, 4)].reshape(span, C)
        occupied = jnp.concatenate([mask[p]] * 4, axis=0)
        sig = sigmoid(pre)
        feature = (occupied * (pre * sig)).astype(BF16)
        slope = occupied * (sig * (1.0 + pre * (1.0 - sig)))
        feat[here, :] = feature
        lines = pl.ds(4 * p, 4)
        m32[lines] = slope.reshape(4, CY, C)
        up = dot(feature, hup[...])
        sig = sigmoid(up)
        hidden = (up * sig).astype(BF16)
        hid[here, :] = hidden
        maps_o[here, :] = dot(hidden, hout[...]).astype(BF16)
        grad = (dot(cot[here, :], hout_t[...]) * (sig * (1.0 + up * (1.0 - sig)))).astype(BF16)
        gh[here, :] = grad
        value = dot(grad, hup_t[...]) * m32[lines].reshape(span, C)
        m32[lines] = value.reshape(4, CY, C)
        gp[here, :] = value.astype(BF16)
        return 0

    lax.fori_loop(0, d.tx, forward, 0, unroll=True)
    halo_start(1)
    term = dot_tn(feat[...], gh[...])
    for half in range(d.head // C):
        h32[half * C : (half + 1) * C, :] = term[:, half * C : (half + 1) * C]
    base = d.head
    term = dot_tn(hid[...], cot[...])
    depth = d.head // 2
    for half in range(2):
        h32[base : base + depth, half * d.outc : (half + 1) * d.outc] = term[
            half * depth : (half + 1) * depth, :
        ]
    hb[...] = h32[...].astype(BF16)
    hmine = pl.ds(pl.multiple_of(core * d.hc, d.hc), d.hc)
    htheirs = pl.ds(pl.multiple_of((1 - core) * d.hc, d.hc), d.hc)
    hcore_copy = rcopy(hb.at[htheirs], hcore_r, core_send.at[1], core_recv.at[1], other_core)
    hcore_copy.start()

    def tap_grads(i, _):
        for j in range(3):
            term = dot_tn(
                m3[pl.ds(pl.multiple_of(i * CY, CY), d.cells), j * C : (j + 1) * C], gp[...]
            )
            at = pl.ds(pl.multiple_of(i * (3 * C) + j * C, C), C)
            dw32[at, :] = term
        return 0

    lax.fori_loop(0, 3, tap_grads, 0)
    for k in range(d.units):
        theirs = pl.ds(pl.multiple_of((2 * k + 1 - core) * d.u, 8), d.u)
        dwb[k, 0 : d.u, :] = dw32[theirs, :].astype(BF16)
    core_copy = rcopy(dwb, core_r, core_send.at[0], core_recv.at[0], other_core)
    core_copy.start()

    hcore_copy.wait_recv()
    hs32[...] = h32[hmine, :] + hcore_r[...].astype(F32)
    for k in range(X):
        hxs[k] = hs32[k * d.hx : (k + 1) * d.hx, :].astype(BF16)
    hx_wait = send_all(hxs, hx_r, X, s, x_peer, hx_send, hx_recv)

    halo_inner(g3)
    conv_inner(g3, wt)

    hx_wait.wait_recv()
    total = hs32[pl.ds(pl.multiple_of(s * d.hx, d.hx), d.hx), :]
    for k in range(X - 1):
        total = total + hx_r[k].astype(F32)
    hxsum[0 : d.hx, :] = total
    for k in range(Z):
        part = hxsum[k * d.hz : k * d.hz + d.hzp, :]
        hzs32[k] = part
        hzs[k] = part.astype(BF16)
    hz_wait = send_all(hzs, hz_r, Z, z, z_peer, hz_send, hz_recv)

    core_copy.wait_recv()
    for k in range(d.units):
        mine = pl.ds(pl.multiple_of((2 * k + core) * d.u, 8), d.u)
        cs32[k * d.u : (k + 1) * d.u, :] = dw32[mine, :] + core_r[k, 0 : d.u, :].astype(F32)
    for k in range(X):
        bx[k] = cs32[k * d.bx : (k + 1) * d.bx, :].astype(BF16)
    bx_wait = send_all(bx, bx_r, X, s, x_peer, bx_send, bx_recv)

    halo_finish(1, g3, False)
    conv_edges(1, g3, wt)

    def backward(p, _):
        here = pl.ds(pl.multiple_of(p * span, span), span)
        acc = conv[pl.ds(4 * p, 4)].reshape(span, C)
        acc = acc * jnp.concatenate([mask[p]] * 4, axis=0)
        gin_o[here, :] = acc.astype(BF16)
        m32[pl.ds(4 * p, 4)] = acc.reshape(4, CY, C)
        for q in range(d.ty):
            parts = [m32[4 * p + dx, 4 * q : 4 * q + 4, :] for dx in range(4)]
            tiles[p * d.ty + q] = jnp.concatenate(parts, axis=0).astype(BF16)
        return 0

    lax.fori_loop(0, d.tx, backward, 0, unroll=True)
    hz_wait.wait_recv()
    total = hzs32[z]
    for k in range(Z - 1):
        total = total + hz_r[k].astype(F32)
    hy[...] = total.astype(BF16)
    for k in range(1, Y):
        rcopy(hy, hy_r.at[k - 1], hy_send, hy_recv, y_peer(k)).start()
    hy_wait = rcopy(hy_r, hy_r, hy_send, hy_recv, other_core)

    def b_start(far, step):
        to, device = a_peer(far, step)
        for slot in range(2):
            ret[to, slot] = tiles[inv[0, to * 2 + slot]]
        rcopy(ret.at[to], gcam_o.at[me], b_send, b_recv, device).start()

    for step in range(2):
        for far in order:
            if far or step:
                b_start(far, step)
    for slot in range(2):
        ret[me, slot] = tiles[inv[0, me * 2 + slot]]
    own_out = pltpu.make_async_copy(ret.at[me], gcam_o.at[me], out_sem)
    own_out.start()

    hy_wait.wait_recv()
    total = hy[...].astype(F32)
    for k in range(Y - 1):
        total = total + hy_r[k].astype(F32)
    hpart[z] = total.astype(BF16)
    part = hpart.at[z]
    for k in range(1, Z):
        rcopy(part, part, gz_send, gz_recv, z_peer(k)).start()

    bx_wait.wait_recv()
    total = cs32[pl.ds(pl.multiple_of(s * d.bx, 8), d.bx), :]
    for k in range(X - 1):
        total = total + bx_r[k].astype(F32)
    bxsum[0 : d.bx, :] = total
    for k in range(Z):
        for y in range(d.YL):
            here = y * d.u + k * d.uz
            bz32[k, y * d.uz : (y + 1) * d.uz, :] = bxsum[here : here + d.uz, :]
        bz[k] = bz32[k].astype(BF16)
    bz_wait = send_all(bz, bz_r, Z, z, z_peer, bz_send, bz_recv)

    def b_rest(step, _):
        for far in order:
            b_start(far, step)
        return 0

    lax.fori_loop(2, 2 * X, b_rest, 0)

    parts = hpart.at[pl.ds(0, Z - 1)]
    gz_wait = rcopy(parts, parts, gz_send, gz_recv, other_core)
    gz_wait.wait_recv()
    for k in range(Z):
        hpack[k * d.hz : k * d.hz + d.hzp, :] = hpart[k].astype(F32)
    hall[core * X + s] = hpack[0 : d.hx, :].astype(BF16)
    part = hall.at[core * X + s]
    for k in range(1, X):
        rcopy(part, part, gx_send, gx_recv, x_peer(k)).start()
    for k in range(X):
        across = ((s + k) % X, yl * 2 + 1 - core, r)
        rcopy(part, part, gx_send, gx_recv, across).start()

    bz_wait.wait_recv()
    total = bz32[z]
    for k in range(Z - 1):
        total = total + bz_r[k].astype(F32)
    brow[pl.ds(0, d.rlp, stride=2), :] = total[:, 0:128]
    brow[pl.ds(1, d.rlp, stride=2), :] = total[:, 128:256]
    for k in range(Y):
        part = brow[k * d.hb : k * d.hb + d.hbp, :]
        l32[k] = part
        ls[k] = part.astype(BF16)
    l_wait = send_all(ls, l_r, Y, my_y, y_peer, l_send, l_recv)

    parts = hall.at[pl.ds(0, 2 * X - 1)]
    gx_wait = rcopy(parts, parts, gx_send, gx_recv, other_core)

    l_wait.wait_recv()
    total = l32[my_y]
    for k in range(Y - 1):
        total = total + l_r[k].astype(F32)
    gconv_o[...] = total[0 : d.hb, :] * d.scale

    gx_wait.wait_recv()
    for c in range(2):
        for x in range(X):
            at = c * d.hc + x * d.hx
            h32[at : at + d.hx, :] = hall[c * X + x].astype(F32)
    for half in range(d.head // C):
        gup_o[:, half * C : (half + 1) * C] = h32[half * C : (half + 1) * C, :] * d.scale
    for half in range(2):
        gout_o[half * depth : (half + 1) * depth, :] = (
            h32[base : base + depth, half * d.outc : (half + 1) * d.outc] * d.scale
        )

    parts = ret.at[all_but_one]
    b_wait = rcopy(parts, gcam_o.at[all_but_one], b_send, b_recv, other_core)
    b_wait.wait_recv()

    rcopy(parts, parts, a_send, a_recv, other_core).wait_send()
    b_wait.wait_send()
    for k in range(2):
        rcopy(rows_s.at[k], rows_r.at[k], row_send.at[k], row_recv.at[k], other_core).wait_send()
        rcopy(cols_r.at[k], cols_r.at[k], col_send.at[k], col_recv.at[k], other_core).wait_send()
    for wait in (
        bx_wait, bz_wait, hx_wait, hz_wait, hy_wait, gz_wait, gx_wait,
        l_wait, core_copy, hcore_copy,
    ):
        wait.wait_send()

    own_out.wait()


def copy_kernel(*refs):
    stores = [
        pltpu.make_async_copy(refs[k], refs[6 + k], refs[12].at[k]) for k in range(6)
    ]
    for store in stores:
        store.start()
    for store in stores:
        store.wait()


def per_device(
    cam_send, lidar_bev, tile_active, tile_source, conv_weight, head_up, head_out, cotangent
):
    channels = cam_send.shape[5]
    cells_x, cells_y = lidar_bev.shape[1], lidar_bev.shape[2]
    head, outc = head_out.shape
    d = Dims(
        lax.axis_size("src"), lax.axis_size("gx"), lax.axis_size("gy"),
        cells_x, cells_y, channels, head, outc,
    )
    C, X, Y, Z, N = d.c, d.X, d.Y, d.Z, d.N
    cells = d.cells
    vmem = pl.BlockSpec(memory_space=pltpu.VMEM)
    anyw = pl.BlockSpec(memory_space=pl.ANY)
    dma = pltpu.SemaphoreType.DMA

    def b16(*shape):
        return pltpu.VMEM(shape, BF16)

    def f32(*shape):
        return pltpu.VMEM(shape, F32)

    def i32(*shape):
        return pltpu.VMEM(shape, jnp.int32)

    scratch = [
        b16(N, 2, 16, C), b16(cells, C), b16(3, 3 * C, C), b16(C, head), b16(head, outc),
        b16(cells, outc), i32(d.tx, d.ty), i32(d.tx, d.ty), pltpu.SMEM((d.tx, d.ty), jnp.int32),
        i32(8, 128), pltpu.SMEM((8, 128), jnp.int32),
        b16(3, 3 * C, C), b16(head, C), b16(outc, head), f32(d.tx, cells_y, C),
        f32(cells_x, cells_y, C), f32(cells_x, cells_y, C),
        b16((cells_x + 2) * cells_y, 3 * C), b16((cells_x + 2) * cells_y, 3 * C),
        b16(2, 2, cells_y, C), b16(2, 2, cells_y, C),
        b16(2, 2, d.colp, C), b16(2, 2, 3, d.colp, C),
        b16(cells, C), b16(cells, head), b16(cells, head), b16(cells, C),
        b16(d.tiles, 16, C), b16(N, 2, 16, C),
        f32(d.rows, C), b16(d.units, d.up, C), b16(d.units, d.up, C), f32(d.rc, C),
        b16(X, d.bx, C), b16(X - 1, d.bx, C), f32(d.bx + d.rlp, C),
        f32(Z, d.rlp, C), b16(Z, d.rlp, C), b16(Z - 1, d.rlp, C), f32(2 * d.rlp + 16, 128),
        f32(Y, d.hbp, 128), b16(Y, d.hbp, 128), b16(Y - 1, d.hbp, 128),
        f32(d.hrows, C), b16(d.hrows, C), b16(d.hc, C), f32(d.hc, C),
        b16(X, d.hx, C), b16(X - 1, d.hx, C), f32(d.hx + 16, C),
        f32(Z, d.hzp, C), b16(Z, d.hzp, C), b16(Z - 1, d.hzp, C),
        b16(d.hzp, C), b16(Y - 1, d.hzp, C),
        b16(Z, d.hzp, C), f32(d.hx + 16, C), b16(2 * X, d.hx, C),
        dma((9,)), dma,
        dma, dma, dma, dma, dma((2,)), dma((2,)), dma((2,)), dma((2,)), dma((2,)), dma((2,)),
        *[dma] * 16,
    ]
    results = pl.pallas_call(
        functools.partial(kernel, d),
        out_shape=(
            pltpu.VMEM((cells, outc), BF16),
            pltpu.VMEM((cells, C), BF16),
            pltpu.VMEM((N, 2, 16, C), BF16),
            pltpu.VMEM((d.hb, 128), F32),
            pltpu.VMEM((C, head), F32),
            pltpu.VMEM((head, outc), F32),
        ),
        in_specs=[anyw] * 8,
        out_specs=(vmem,) * 6,
        scratch_shapes=scratch,
        compiler_params=pltpu.CompilerParams(
            collective_id=0, has_side_effects=True, vmem_limit_bytes=VMEM_BYTES
        ),
    )(
        cam_send.reshape(N, 2, 16, C),
        lidar_bev.reshape(cells, C),
        tile_active.reshape(d.tx, d.ty),
        tile_source.reshape(d.tx, d.ty),
        conv_weight.reshape(3, 3 * C, C),
        head_up,
        head_out,
        cotangent.reshape(cells, outc),
    )
    maps, gin, gcam, gconv, gup, gout = pl.pallas_call(
        copy_kernel,
        out_shape=tuple(jax.ShapeDtypeStruct(a.shape, a.dtype) for a in results),
        in_specs=[vmem] * 6,
        out_specs=(anyw,) * 6,
        scratch_shapes=[dma((6,))],
        compiler_params=pltpu.CompilerParams(vmem_limit_bytes=1024 * 1024),
    )(*results)
    return (
        maps.reshape(1, cells_x, cells_y, outc),
        gin.reshape(1, cells_x, cells_y, C),
        gcam.reshape(1, 1, N, 2, 16, C),
        gconv.reshape(-1),
        gup,
        gout,
    )


def solution(mesh):
    in_specs = (
        P(("src", "gx"), "gy", None, None, None, None),
        P("src", "gx", "gy", None),
        P("src", "gx", "gy"),
        P("src", "gx", "gy"),
        P(),
        P(),
        P(),
        P("src", "gx", "gy", None),
    )
    out_specs = (
        P("src", "gx", "gy", None),
        P("src", "gx", "gy", None),
        P(("src", "gx"), "gy", None, None, None, None),
        P(("src", "gx", "gy")),
        P(),
        P(),
    )
    return jax.shard_map(
        per_device, mesh=mesh, in_specs=in_specs, out_specs=out_specs, check_vma=False
    )
```
